32 devices in a mesh: row: 4 (over y, x), col: 8 (over z, core).
Axes of the slice: x: 2, y: 2, z: 4, core: 2. Of those that a mesh axis runs over, the one named last changes fastest.
Arguments:
- tokens: bfloat16 [48, 96, 768], P('row', 'col'), may hold values from -6 to 6
- w_in: bfloat16 [768, 1536], replicated, may hold values from -0.21875 to 0.21875
- w_xproj: bfloat16 [768, 80], replicated, may hold values from -0.21875 to 0.21875
- w_dt: bfloat16 [48, 768], replicated, may hold values from -0.875 to 0.875
- dt_bias: float32 [768], replicated, may hold values from -7 to -2.3
- a_log: float32 [16, 768], replicated, may hold values from 0 to 2.77
- d_skip: float32 [768], replicated, may hold values from 0.5 to 1.5
- w_out: bfloat16 [768, 768], replicated, may hold values from -0.21875 to 0.21875
- out_grad: bfloat16 [48, 96, 768], P('row', 'col'), may hold values from -6 to 6
Outputs:
- layer_out: bfloat16 [48, 96, 768], P('row', 'col')
- token_grad: bfloat16 [48, 96, 768], P('row', 'col')
The draws below stay inside these ranges and needn't reach their ends.
All inputs are finite; a program needn't handle non-finite values.
Results may differ from the reference program's by a relative error of at most 0.0064.
Values sent between devices are 32-bit elements; how exact they have to be, the bound alone decides.
A program may use at most 192 MiB of HBM per device.

```python
import jax
import jax.numpy as jnp
from jax import lax

D = 768
STATE = 16
RANK = 48
INNER = 768
ROWS = 48
COLS = 96


def block_scale(stream_key, shape, shards, low, top_value):
    loudness = 1.0
    for position, parts in shards:
        steps = jax.random.uniform(jax.random.fold_in(jax.random.fold_in(stream_key, 6), position), (parts,), jnp.float32, low / len(shards), top_value / len(shards))
        loudness = loudness * jnp.repeat(jnp.exp(steps), shape[position] // parts).reshape((-1,) + (1,) * (len(shape) - 1 - position))
    return loudness


def bell_draw(own_key, extent, deviation, bound, cuts=(), dtype=jnp.bfloat16):
    values = jax.random.normal(own_key, extent, jnp.float32) * deviation
    if len(cuts) > 0:
        values = block_scale(own_key, extent, cuts, -0.22, 0.18) * values
    return jnp.clip(values, min=-bound, max=bound).astype(dtype)


def setup_inputs(seed: int = 0) -> dict:
    key_list = jax.random.split(jax.random.key(seed), 10)
    return {
        "tokens": bell_draw(key_list[0], (ROWS, COLS, D), 1.0, 6.0, ((0, 4), (1, 8))),
        "w_in": bell_draw(key_list[1], (D, 2 * INNER), D ** -0.5, 0.21875),
        "w_xproj": bell_draw(key_list[2], (INNER, RANK + 2 * STATE), INNER ** -0.5, 0.21875),
        "w_dt": bell_draw(key_list[3], (RANK, INNER), RANK ** -0.5, 0.875),
        "dt_bias": jnp.clip(jax.random.uniform(key_list[4], (INNER,), jnp.float32, -7.0, -2.3), -7.0, -2.3),
        "a_log": jnp.clip(jax.random.uniform(key_list[5], (STATE, INNER), jnp.float32, 0.0, 2.77), 0.0, 2.77),
        "d_skip": jnp.clip(jax.random.uniform(key_list[6], (INNER,), jnp.float32, 0.5, 1.5), 0.5, 1.5),
        "w_out": bell_draw(key_list[7], (INNER, D), INNER ** -0.5, 0.21875),
        "out_grad": bell_draw(key_list[8], (ROWS, COLS, D), 1.0, 6.0, ((0, 4), (1, 8))),
    }


channel_block = 16

def compose(earlier, later):
    return (earlier[0] * later[0], later[0] * earlier[1] + later[1])

def silu_grad(values):
    sigmoid = jax.nn.sigmoid(values)
    return sigmoid * (1.0 + values * (1.0 - sigmoid))

def reference(tokens, w_in, w_xproj, w_dt, dt_bias, a_log, d_skip, w_out, out_grad):
    grid_rows, grid_cols, model_width = tokens.shape
    cell_count = grid_rows * grid_cols
    low_rank, inner_width = w_dt.shape
    states = a_log.shape[0]
    flat_tokens = tokens.reshape(cell_count, model_width)
    projected = jnp.dot(flat_tokens, w_in, preferred_element_type=jnp.float32)
    x_pre = projected[:, :inner_width]
    z_pre = projected[:, inner_width:]
    x_act = jax.nn.silu(x_pre).astype(jnp.bfloat16)
    x_dbl = jnp.dot(x_act, w_xproj, preferred_element_type=jnp.float32)
    dt_low = x_dbl[:, :low_rank].astype(jnp.bfloat16)
    b_sel = x_dbl[:, low_rank:low_rank + states]
    c_sel = x_dbl[:, low_rank + states:]
    dt_pre = jnp.dot(dt_low, w_dt, preferred_element_type=jnp.float32) + dt_bias
    step_size = jax.nn.softplus(dt_pre)
    gated_grad = jnp.dot(out_grad.reshape(cell_count, model_width), w_out.T, preferred_element_type=jnp.float32)
    z_silu = jax.nn.silu(z_pre)
    scan_grad = gated_grad * z_silu
    rates = -jnp.exp(a_log)
    step_grid = step_size.reshape(grid_rows, grid_cols, inner_width)
    x_grid = x_act.astype(jnp.float32).reshape(grid_rows, grid_cols, inner_width)
    grad_grid = scan_grad.reshape(grid_rows, grid_cols, inner_width)
    b_grid = b_sel.reshape(grid_rows, grid_cols, states)
    c_grid = c_sel.reshape(grid_rows, grid_cols, states)

    def one_block(block_index, carry):
        scan_out, step_grad, xscan_grad, bsel_grad, csel_grad = carry
        first_channel = (block_index * channel_block).astype(jnp.int32)
        step_part = lax.dynamic_slice_in_dim(step_grid, first_channel, channel_block, 2)
        x_part = lax.dynamic_slice_in_dim(x_grid, first_channel, channel_block, 2)
        grad_part = lax.dynamic_slice_in_dim(grad_grid, first_channel, channel_block, 2)
        rate_part = lax.dynamic_slice_in_dim(rates, first_channel, channel_block, 1)
        skip_part = lax.dynamic_slice_in_dim(d_skip, first_channel, channel_block, 0)
        decays = jnp.exp(step_part[:, :, None, :] * rate_part)
        source = step_part[:, :, None, :] * b_grid[:, :, :, None] * x_part[:, :, None, :]
        row_state = lax.associative_scan(compose, (decays, source), axis=1)[1]
        full_state = lax.associative_scan(compose, (decays, row_state), axis=0)[1]
        out_part = lax.optimization_barrier(jnp.sum(c_grid[:, :, :, None] * full_state, axis=2)) + skip_part * x_part
        state_grad = c_grid[:, :, :, None] * grad_part[:, :, None, :]
        csel_grad = csel_grad + lax.optimization_barrier(jnp.sum(grad_part[:, :, None, :] * full_state, axis=3))
        col_shift = jnp.concatenate([decays[1:], jnp.ones_like(decays[:1])], axis=0)
        col_adjoint = lax.associative_scan(compose, (col_shift, state_grad), axis=0, reverse=True)[1]
        row_shift = jnp.concatenate([decays[:, 1:], jnp.ones_like(decays[:, :1])], axis=1)
        row_adjoint = lax.associative_scan(compose, (row_shift, col_adjoint), axis=1, reverse=True)[1]
        col_before = jnp.concatenate([jnp.zeros_like(full_state[:1]), full_state[:-1]], axis=0)
        row_before = jnp.concatenate([jnp.zeros_like(row_state[:, :1]), row_state[:, :-1]], axis=1)
        decay_grad = col_adjoint * col_before + row_adjoint * row_before
        step_part_grad = lax.optimization_barrier(jnp.sum(decay_grad * decays * rate_part + row_adjoint * b_grid[:, :, :, None] * x_part[:, :, None, :], axis=2))
        bsel_grad = bsel_grad + lax.optimization_barrier(jnp.sum(row_adjoint * step_part[:, :, None, :] * x_part[:, :, None, :], axis=3))
        xscan_part = lax.optimization_barrier(jnp.sum(row_adjoint * step_part[:, :, None, :] * b_grid[:, :, :, None], axis=2)) + grad_part * skip_part
        scan_out = lax.dynamic_update_slice_in_dim(scan_out, out_part, first_channel, 2)
        step_grad = lax.dynamic_update_slice_in_dim(step_grad, step_part_grad, first_channel, 2)
        xscan_grad = lax.dynamic_update_slice_in_dim(xscan_grad, xscan_part, first_channel, 2)
        return (scan_out, step_grad, xscan_grad, bsel_grad, csel_grad)
    wide_zero = jnp.zeros((grid_rows, grid_cols, inner_width), jnp.float32)
    narrow_zero = jnp.zeros((grid_rows, grid_cols, states), jnp.float32)
    scan_out, step_grad, xscan_grad, bsel_grad, csel_grad = lax.fori_loop(0, inner_width // channel_block, one_block, (wide_zero, wide_zero, wide_zero, narrow_zero, narrow_zero))
    scan_flat = scan_out.reshape(cell_count, inner_width)
    gated_out = (scan_flat * z_silu).astype(jnp.bfloat16)
    layer_out = jnp.dot(gated_out, w_out, preferred_element_type=jnp.float32).astype(jnp.bfloat16)
    z_grad = gated_grad * scan_flat * silu_grad(z_pre)
    pre_grad = (step_grad.reshape(cell_count, inner_width) * jax.nn.sigmoid(dt_pre)).astype(jnp.bfloat16)
    low_grad = jnp.dot(pre_grad, w_dt.T, preferred_element_type=jnp.float32)
    dbl_grad = jnp.concatenate([low_grad, bsel_grad.reshape(cell_count, states), csel_grad.reshape(cell_count, states)], axis=1).astype(jnp.bfloat16)
    x_grad = xscan_grad.reshape(cell_count, inner_width) + jnp.dot(dbl_grad, w_xproj.T, preferred_element_type=jnp.float32)
    proj_grad = jnp.concatenate([x_grad * silu_grad(x_pre), z_grad], axis=1).astype(jnp.bfloat16)
    token_grad = jnp.dot(proj_grad, w_in.T, preferred_element_type=jnp.float32).astype(jnp.bfloat16)
    return (layer_out.reshape(grid_rows, grid_cols, model_width), token_grad.reshape(grid_rows, grid_cols, model_width))
```

```python
import functools
import math

import jax
import jax.numpy as jnp
from jax import lax
from jax.experimental import pallas as pl
from jax.experimental.pallas import tpu as pltpu
from jax.sharding import PartitionSpec as P

MESH = pl.DeviceIdType.MESH
LANES = 128
F32 = jnp.float32


def silu_grad(values):
    sigmoid = jax.nn.sigmoid(values)
    return sigmoid * (1.0 + values * (1.0 - sigmoid))


def dot_transposed(left, right):
    return lax.dot_general(
        left, right, (((1,), (1,)), ((), ())), preferred_element_type=jnp.float32
    )


def scan_kernel(
    sizes,
    step_ref, u_ref, g_ref, rate_ref, b_ref, c_ref, rsum_ref, csum_ref,
    out_ref, rb_ref, sd_ref, bacc_ref, cacc_ref,
    decay, rows, cols, prow, pcol,
    e1r, e1c, e2r, e2c, in1r, in1c, in2r, in2c, fcar,
    send_sem, recv_sem,
):
    n_row, n_col, tr, tc, chunks, states = sizes
    r = lax.axis_index("row")
    p = lax.axis_index("col")
    left, right = (r, lax.rem(p + n_col - 1, n_col)), (r, lax.rem(p + 1, n_col))
    up, down = (lax.rem(r + n_row - 1, n_row), p), (lax.rem(r + 1, n_row), p)
    first_col, last_col = p == 0, p == n_col - 1
    first_row, last_row = r == 0, r == n_row - 1

    barrier = pltpu.get_barrier_semaphore()
    edges = ((first_col, left), (last_col, right), (first_row, up), (last_row, down))
    for edge, neighbour in edges:
        @pl.when(jnp.logical_not(edge))
        def _():
            pl.semaphore_signal(barrier, inc=1, device_id=neighbour, device_id_type=MESH)
    peers = sum(jnp.where(edge, 0, 1) for edge, _ in edges)
    pl.semaphore_wait(barrier, peers)

    links = (
        (e1r, in1r, right, first_col, last_col, prow),
        (e1c, in1c, up, last_row, first_row, pcol),
        (e2c, in2c, down, first_row, last_row, pcol),
        (e2r, in2r, left, last_col, first_col, prow),
    )

    def copy(kind, k):
        source, target, where = links[kind][:3]
        return pltpu.make_async_remote_copy(
            src_ref=source.at[k],
            dst_ref=target.at[k],
            send_sem=send_sem.at[kind, k],
            recv_sem=recv_sem.at[kind, k],
            device_id=where,
            device_id_type=MESH,
        )

    for kind in range(4):
        @pl.when(links[kind][3])
        def _():
            links[kind][1][...] = jnp.zeros_like(links[kind][1])

    def head_send(kind, k):
        head, tail = links[kind][3:5]

        @pl.when(jnp.logical_and(head, jnp.logical_not(tail)))
        def _():
            copy(kind, k).start()

    def forward(kind, k):
        source, target, _, head, tail, product = links[kind]

        @pl.when(jnp.logical_not(head))
        def _():
            copy(kind, k).wait_recv()

        @pl.when(jnp.logical_not(jnp.logical_or(head, tail)))
        def _():
            source[k] = source[k] + product[k] * target[k]
            copy(kind, k).start()

    def lanes(k):
        return pl.ds(pl.multiple_of(k * LANES, LANES), LANES)

    zero = jnp.zeros((states, LANES), F32)

    @pl.loop(0, chunks)
    def _(k):
        cut = lanes(k)
        rate = rate_ref[:, cut]
        for i in range(tr):
            prow[k, i] = jnp.exp2(rate * rsum_ref[i : i + 1, cut])
        for j in range(tc):
            pcol[k, j] = jnp.exp2(rate * csum_ref[j : j + 1, cut])

        def line(count, terms):
            i = tr - 1 - count
            state = zero
            after = []
            for j in range(tc):
                t = i * tc + j
                d = jnp.exp2(rate * step_ref[i, j : j + 1, cut])
                decay[k, t] = d
                state = d * state + u_ref[i, j : j + 1, cut] * b_ref[t]
                after.append(d * (terms[j] + g_ref[i, j : j + 1, cut] * c_ref[t]))
            e1r[k, i] = state
            return tuple(after)

        terms = lax.fori_loop(0, tr, line, (zero,) * tc)
        for j in range(tc):
            e1c[k, j] = terms[j]
        head_send(0, k)
        head_send(1, k)

    @pl.loop(0, chunks)
    def _(k):
        cut = lanes(k)
        forward(0, k)
        forward(1, k)

        def down_line(i, states_in):
            state = in1r[k, i]
            after = []
            for j in range(tc):
                t = i * tc + j
                d = decay[k, t]
                state = d * state + u_ref[i, j : j + 1, cut] * b_ref[t]
                rows[k, t] = state
                after.append(d * states_in[j] + state)
            return tuple(after)

        ends = lax.fori_loop(0, tr, down_line, (zero,) * tc)
        for j in range(tc):
            e2c[k, j] = ends[j]
        head_send(2, k)

        def up_line(count, terms):
            i = tr - 1 - count
            term = zero
            after = [None] * tc
            for j in reversed(range(tc)):
                t = i * tc + j
                d = decay[k, t]
                adjoint = terms[j] + g_ref[i, j : j + 1, cut] * c_ref[t]
                cols[k, t] = adjoint
                after[j] = d * adjoint
                term = d * (adjoint + term)
            e2r[k, i] = term
            return tuple(after)

        lax.fori_loop(0, tr, up_line, tuple(in1c[k, j] for j in range(tc)))
        head_send(3, k)

    bacc_ref[...] = jnp.zeros_like(bacc_ref)
    cacc_ref[...] = jnp.zeros_like(cacc_ref)

    @pl.loop(0, chunks)
    def _(k):
        cut = lanes(k)
        rate = rate_ref[:, cut]
        forward(2, k)
        forward(3, k)
        for j in range(tc):
            fcar[j] = in2c[k, j]

        def last_line(i, carry):
            term = in2r[k, i]
            for j in reversed(range(tc)):
                t = i * tc + j
                d = decay[k, t]
                adjoint = cols[k, t]
                state = rows[k, t]
                before = in1r[k, i] if j == 0 else rows[k, t - 1]
                passed = d * fcar[j]
                full = passed + state
                fcar[j] = full
                total = adjoint + term
                term = d * total
                slope = adjoint * passed + term * before
                sd_ref[i, j : j + 1, cut] = jnp.sum(slope * rate, axis=0, keepdims=True)
                rb_ref[i, j : j + 1, cut] = jnp.sum(total * b_ref[t], axis=0, keepdims=True)
                out_ref[i, j : j + 1, cut] = jnp.sum(full * c_ref[t], axis=0, keepdims=True)
                bacc_ref[t] += total * u_ref[i, j : j + 1, cut]
                cacc_ref[t] += full * g_ref[i, j : j + 1, cut]
            return carry

        lax.fori_loop(0, tr, last_line, 0)

    for kind in range(4):
        tail = links[kind][4]

        @pl.when(jnp.logical_not(tail))
        def _():
            @pl.loop(0, chunks)
            def _(k):
                copy(kind, k).wait_send()


def scans(mesh_shape, tr, tc, step, u, g, rate, b_wide, c_wide, rsum, csum):
    cells, width = tr * tc, step.shape[-1]
    states = rate.shape[0]
    chunks = width // LANES
    sizes = (mesh_shape["row"], mesh_shape["col"], tr, tc, chunks, states)
    grid_buf = pltpu.VMEM((chunks, cells, states, LANES), F32)
    row_buf = pltpu.VMEM((chunks, tr, states, LANES), F32)
    col_buf = pltpu.VMEM((chunks, tc, states, LANES), F32)
    wide = jax.ShapeDtypeStruct((tr, tc, width), F32)
    acc = jax.ShapeDtypeStruct((cells, states, LANES), F32)
    return pl.pallas_call(
        functools.partial(scan_kernel, sizes),
        out_shape=(wide, wide, wide, acc, acc),
        in_specs=[pl.BlockSpec(memory_space=pltpu.VMEM)] * 8,
        out_specs=(pl.BlockSpec(memory_space=pltpu.VMEM),) * 5,
        scratch_shapes=[
            grid_buf, grid_buf, grid_buf, row_buf, col_buf,
            row_buf, col_buf, row_buf, col_buf, row_buf, col_buf, row_buf, col_buf,
            pltpu.VMEM((tc, states, LANES), F32),
            pltpu.SemaphoreType.DMA((4, chunks)),
            pltpu.SemaphoreType.DMA((4, chunks)),
        ],
        compiler_params=pltpu.CompilerParams(
            collective_id=0, has_side_effects=True, vmem_limit_bytes=56 * 1024 * 1024
        ),
    )(step, u, g, rate, b_wide, c_wide, rsum, csum)


def body(mesh_shape, tokens, w_in, w_xproj, w_dt, dt_bias, a_log, d_skip, w_out, out_grad):
    tile_rows, tile_cols, model_width = tokens.shape
    cell_count = tile_rows * tile_cols
    low_rank, inner_width = w_dt.shape
    states = a_log.shape[0]
    flat_tokens = tokens.reshape(cell_count, model_width)
    projected = jnp.dot(flat_tokens, w_in, preferred_element_type=jnp.float32)
    x_pre = projected[:, :inner_width]
    z_pre = projected[:, inner_width:]
    x_act = jax.nn.silu(x_pre).astype(jnp.bfloat16)
    x_dbl = jnp.dot(x_act, w_xproj, preferred_element_type=jnp.float32)
    dt_low = x_dbl[:, :low_rank].astype(jnp.bfloat16)
    b_sel = x_dbl[:, low_rank : low_rank + states]
    c_sel = x_dbl[:, low_rank + states :]
    dt_pre = jnp.dot(dt_low, w_dt, preferred_element_type=jnp.float32) + dt_bias
    step_size = jax.nn.softplus(dt_pre)
    gated_grad = dot_transposed(out_grad.reshape(cell_count, model_width), w_out)
    z_silu = jax.nn.silu(z_pre)
    scan_grad = gated_grad * z_silu
    x_wide = x_act.astype(F32)
    step_grid = step_size.reshape(tile_rows, tile_cols, inner_width)
    shape = (cell_count, states, LANES)
    grid = (tile_rows, tile_cols, inner_width)
    cf, rb, slope, bacc, cacc = scans(
        mesh_shape, tile_rows, tile_cols,
        step_grid, (step_size * x_wide).reshape(grid), scan_grad.reshape(grid), -jnp.exp(a_log) * math.log2(math.e),
        jnp.broadcast_to(b_sel[:, :, None], shape), jnp.broadcast_to(c_sel[:, :, None], shape),
        jnp.sum(step_grid, axis=1), jnp.sum(step_grid, axis=0),
    )
    cf, rb, slope = (a.reshape(cell_count, inner_width) for a in (cf, rb, slope))
    scan_out = cf + d_skip * x_wide
    step_grad = slope * math.log(2.0) + rb * x_wide
    xscan_grad = rb * step_size + scan_grad * d_skip
    gated_out = (scan_out * z_silu).astype(jnp.bfloat16)
    layer_out = jnp.dot(gated_out, w_out, preferred_element_type=jnp.float32).astype(jnp.bfloat16)
    z_grad = gated_grad * scan_out * silu_grad(z_pre)
    pre_grad = (step_grad * jax.nn.sigmoid(dt_pre)).astype(jnp.bfloat16)
    low_grad = dot_transposed(pre_grad, w_dt)
    dbl_grad = jnp.concatenate(
        [low_grad, jnp.sum(bacc, axis=2), jnp.sum(cacc, axis=2)], axis=1
    ).astype(jnp.bfloat16)
    x_grad = xscan_grad + dot_transposed(dbl_grad, w_xproj)
    proj_grad = jnp.concatenate([x_grad * silu_grad(x_pre), z_grad], axis=1).astype(jnp.bfloat16)
    token_grad = dot_transposed(proj_grad, w_in).astype(jnp.bfloat16)
    return (
        layer_out.reshape(tile_rows, tile_cols, model_width),
        token_grad.reshape(tile_rows, tile_cols, model_width),
    )


def solution(mesh):
    return jax.shard_map(
        functools.partial(body, dict(mesh.shape)),
        mesh=mesh,
        in_specs=(P("row", "col", None), P(), P(), P(), P(), P(), P(), P(), P("row", "col", None)),
        out_specs=(P("row", "col", None), P("row", "col", None)),
        check_vma=False,
    )
```

```python
import functools
import math

import jax
import jax.numpy as jnp
from jax import lax
from jax.experimental import pallas as pl
from jax.experimental.pallas import tpu as pltpu
from jax.sharding import PartitionSpec as P

MESH = pl.DeviceIdType.MESH
LANES = 128
BLOCK = 256
F32 = jnp.float32
BF16 = jnp.bfloat16


def sigmoid(values):
    return 1.0 / (1.0 + jnp.exp(-values))


def silu_grad(values):
    gate = sigmoid(values)
    return gate * (1.0 + values * (1.0 - gate))


def dot(left, right):
    return jnp.dot(left, right, preferred_element_type=F32)


def dot_transposed(left, right):
    return lax.dot_general(left, right, (((1,), (1,)), ((), ())), preferred_element_type=F32)


def layer_kernel(
    sizes,
    tokens_ref, w_in_ref, w_xproj_ref, w_dt_ref, bias_ref, a_log_ref, skip_ref, w_out_ref, grad_ref,
    layer_ref, token_grad_ref,
    pad_ref, x_pre_ref, z_pre_ref, x_ref, step_ref, u_ref, g_ref, gated_ref, dt_ref,
    out_ref, rb_ref, sd_ref, proj_ref, xd_ref, b_ref, c_ref, bacc_ref, cacc_ref,
    decay, rows, cols, prow, pcol,
    e1r, e1c, e2r, e2c, in1r, in1c, in2r, in2c, fcar,
    send_sem, recv_sem,
):
    n_row, n_col, tr, tc, chunks, states, rank = sizes
    pad = pad_ref.shape[1]
    cells = tr * pad
    width = x_ref.shape[-1]
    model = pad_ref.shape[-1]
    r = lax.axis_index("row")
    p = lax.axis_index("col")
    left, right = (r, lax.rem(p + n_col - 1, n_col)), (r, lax.rem(p + 1, n_col))
    up, down = (lax.rem(r + n_row - 1, n_row), p), (lax.rem(r + 1, n_row), p)
    first_col, last_col = p == 0, p == n_col - 1
    first_row, last_row = r == 0, r == n_row - 1

    barrier = pltpu.get_barrier_semaphore()
    edges = ((first_col, left), (last_col, right), (first_row, up), (last_row, down))
    for edge, neighbour in edges:
        @pl.when(jnp.logical_not(edge))
        def _():
            pl.semaphore_signal(barrier, inc=1, device_id=neighbour, device_id_type=MESH)
    peers = sum(jnp.where(edge, 0, 1) for edge, _ in edges)
    pl.semaphore_wait(barrier, peers)

    links = (
        (e1r, in1r, right, first_col, last_col, prow),
        (e1c, in1c, up, last_row, first_row, pcol),
        (e2c, in2c, down, first_row, last_row, pcol),
        (e2r, in2r, left, last_col, first_col, prow),
    )

    def copy(kind, k):
        source, target, where = links[kind][:3]
        return pltpu.make_async_remote_copy(
            src_ref=source.at[k],
            dst_ref=target.at[k],
            send_sem=send_sem.at[kind, k],
            recv_sem=recv_sem.at[kind, k],
            device_id=where,
            device_id_type=MESH,
        )

    for kind in range(4):
        @pl.when(links[kind][3])
        def _():
            links[kind][1][...] = jnp.zeros_like(links[kind][1])

    def head_send(kind, k):
        head, tail = links[kind][3:5]

        @pl.when(jnp.logical_and(head, jnp.logical_not(tail)))
        def _():
            copy(kind, k).start()

    def forward(kind, k):
        source, target, _, head, tail, product = links[kind]

        @pl.when(jnp.logical_not(head))
        def _():
            copy(kind, k).wait_recv()

        @pl.when(jnp.logical_not(jnp.logical_or(head, tail)))
        def _():
            source[k] = source[k] + product[k] * target[k]
            copy(kind, k).start()

    def rates(cut):
        return jnp.exp(a_log_ref[:, cut]) * -math.log2(math.e)

    def lanes(k):
        return pl.ds(pl.multiple_of(k * LANES, LANES), LANES)

    def flat(ref):
        return ref[...].reshape(cells, ref.shape[-1])

    def put(ref, cut, values):
        ref[:, :, cut] = values.reshape(tr, pad, values.shape[-1])

    def get(ref, cut):
        values = ref[:, :, cut]
        return values.reshape(cells, values.shape[-1])

    blocks = [slice(at, at + BLOCK) for at in range(0, width, BLOCK)]
    pad_ref[:, tc:, :] = jnp.zeros((tr, pad - tc, model), F32)
    pad_ref[:, :tc, :] = tokens_ref[...].astype(F32)
    tokens = flat(pad_ref).astype(BF16)
    for cut in blocks:
        x_pre = dot(tokens, w_in_ref[:, cut])
        put(x_pre_ref, cut, x_pre)
        put(x_ref, cut, (x_pre * sigmoid(x_pre)).astype(BF16).astype(F32))
    x_dbl = dot(flat(x_ref).astype(BF16), w_xproj_ref[...])
    xd_ref[:, : rank + 2 * states] = x_dbl
    dt_low = x_dbl[:, :rank].astype(BF16)
    for cut in blocks:
        dt_pre = dot(dt_low, w_dt_ref[:, cut]) + bias_ref[:, cut]
        step = jnp.maximum(dt_pre, 0.0) + jnp.log1p(jnp.exp(-jnp.abs(dt_pre)))
        put(dt_ref, cut, dt_pre)
        put(step_ref, cut, step)
        put(u_ref, cut, step * get(x_ref, cut))
    pad_ref[:, :tc, :] = grad_ref[...].astype(F32)
    grads = flat(pad_ref).astype(BF16)
    for cut in blocks:
        z_pre = dot(tokens, w_in_ref[:, width + cut.start : width + cut.stop])
        gated = dot_transposed(grads, w_out_ref[cut, :])
        put(z_pre_ref, cut, z_pre)
        put(gated_ref, cut, gated)
        put(g_ref, cut, gated * (z_pre * sigmoid(z_pre)))
    for n in range(states):
        spot = pl.ds(n, cells, stride=states)
        for ref, first in ((b_ref, rank), (c_ref, rank + states)):
            column = xd_ref[:, first + n : first + n + 1]
            ref[spot, :] = jnp.broadcast_to(column, (cells, LANES))

    def cell(i, j):
        return pl.ds(pl.multiple_of((i * pad + j) * states, states), states)

    zero = jnp.zeros((states, LANES), F32)

    @pl.loop(0, chunks)
    def _(k):
        cut = lanes(k)
        rate = rates(cut)
        csum = jnp.zeros((pad, LANES), F32)
        for i in range(tr):
            steps = step_ref[i, :, cut]
            csum = csum + steps
            prow[k, i] = jnp.exp2(rate * jnp.sum(steps[:tc], axis=0, keepdims=True))
        for j in range(tc):
            pcol[k, j] = jnp.exp2(rate * csum[j : j + 1])

        def line(count, terms):
            i = tr - 1 - count
            state = zero
            after = []
            for j in range(tc):
                t = i * tc + j
                d = jnp.exp2(rate * step_ref[i, j : j + 1, cut])
                decay[k, t] = d
                state = d * state + u_ref[i, j : j + 1, cut] * b_ref[cell(i, j)]
                after.append(d * (terms[j] + g_ref[i, j : j + 1, cut] * c_ref[cell(i, j)]))
            e1r[k, i] = state
            return tuple(after)

        terms = lax.fori_loop(0, tr, line, (zero,) * tc)
        for j in range(tc):
            e1c[k, j] = terms[j]
        head_send(0, k)
        head_send(1, k)

    @pl.loop(0, chunks)
    def _(k):
        cut = lanes(k)
        forward(0, k)
        forward(1, k)

        def down_line(i, states_in):
            state = in1r[k, i]
            after = []
            for j in range(tc):
                t = i * tc + j
                d = decay[k, t]
                state = d * state + u_ref[i, j : j + 1, cut] * b_ref[cell(i, j)]
                rows[k, t] = state
                after.append(d * states_in[j] + state)
            return tuple(after)

        ends = lax.fori_loop(0, tr, down_line, (zero,) * tc)
        for j in range(tc):
            e2c[k, j] = ends[j]
        head_send(2, k)

        def up_line(count, terms):
            i = tr - 1 - count
            term = zero
            after = [None] * tc
            for j in reversed(range(tc)):
                t = i * tc + j
                d = decay[k, t]
                adjoint = terms[j] + g_ref[i, j : j + 1, cut] * c_ref[cell(i, j)]
                cols[k, t] = adjoint
                after[j] = d * adjoint
                term = d * (adjoint + term)
            e2r[k, i] = term
            return tuple(after)

        lax.fori_loop(0, tr, up_line, tuple(in1c[k, j] for j in range(tc)))
        head_send(3, k)

    bacc_ref[...] = jnp.zeros_like(bacc_ref)
    cacc_ref[...] = jnp.zeros_like(cacc_ref)

    @pl.loop(0, chunks)
    def _(k):
        cut = lanes(k)
        rate = rates(cut)
        forward(2, k)
        forward(3, k)
        for j in range(tc):
            fcar[j] = in2c[k, j]

        def last_line(i, carry):
            term = in2r[k, i]
            for j in reversed(range(tc)):
                t = i * tc + j
                d = decay[k, t]
                adjoint = cols[k, t]
                state = rows[k, t]
                before = in1r[k, i] if j == 0 else rows[k, t - 1]
                passed = d * fcar[j]
                full = passed + state
                fcar[j] = full
                total = adjoint + term
                term = d * total
                slope = adjoint * passed + term * before
                sd_ref[i, j : j + 1, cut] = jnp.sum(slope * rate, axis=0, keepdims=True)
                rb_ref[i, j : j + 1, cut] = jnp.sum(total * b_ref[cell(i, j)], axis=0, keepdims=True)
                out_ref[i, j : j + 1, cut] = jnp.sum(full * c_ref[cell(i, j)], axis=0, keepdims=True)
                bacc_ref[cell(i, j)] += total * u_ref[i, j : j + 1, cut]
                cacc_ref[cell(i, j)] += full * g_ref[i, j : j + 1, cut]
            return carry

        lax.fori_loop(0, tr, last_line, 0)

    both = jnp.zeros((cells, 2 * states), F32)
    lane = lax.broadcasted_iota(jnp.int32, (LANES, 2 * states), 1)
    for n in range(states):
        spot = pl.ds(n, cells, stride=states)
        for ref, at in ((bacc_ref, n), (cacc_ref, states + n)):
            pick = jnp.where(lane == at, 1.0, 0.0).astype(BF16)
            both = both + dot(ref[spot, :].astype(BF16), pick)
    low_grad = jnp.zeros((cells, rank), F32)
    layer = jnp.zeros((cells, model), F32)
    for cut in blocks:
        x, z_pre, dt_pre = get(x_ref, cut), get(z_pre_ref, cut), get(dt_ref, cut)
        scan_out = get(out_ref, cut) + skip_ref[:, cut] * x
        layer = layer + dot((scan_out * (z_pre * sigmoid(z_pre))).astype(BF16), w_out_ref[cut, :])
        put(proj_ref, slice(width + cut.start, width + cut.stop),
            get(gated_ref, cut) * scan_out * silu_grad(z_pre))
        step_grad = get(sd_ref, cut) * math.log(2.0) + get(rb_ref, cut) * x
        low_grad = low_grad + dot_transposed(
            (step_grad * sigmoid(dt_pre)).astype(BF16), w_dt_ref[:, cut]
        )
    layer_ref[...] = layer.reshape(tr, pad, model)[:, :tc, :].astype(BF16)
    xd_ref[:, :rank] = low_grad
    xd_ref[:, rank : rank + 2 * states] = both
    dbl_grad = xd_ref[:, : rank + 2 * states].astype(BF16)
    for cut in blocks:
        x_grad = (
            get(rb_ref, cut) * get(step_ref, cut) + get(g_ref, cut) * skip_ref[:, cut]
            + dot_transposed(dbl_grad, w_xproj_ref[cut, :])
        )
        put(proj_ref, cut, x_grad * silu_grad(get(x_pre_ref, cut)))
    proj = flat(proj_ref).astype(BF16)
    for at in range(0, model, BLOCK):
        token_grad = dot_transposed(proj, w_in_ref[at : at + BLOCK, :])
        token_grad_ref[:, :, at : at + BLOCK] = (
            token_grad.reshape(tr, pad, BLOCK)[:, :tc, :].astype(BF16)
        )

    for kind in range(4):
        tail = links[kind][4]

        @pl.when(jnp.logical_not(tail))
        def _():
            @pl.loop(0, chunks)
            def _(k):
                copy(kind, k).wait_send()


def body(mesh_shape, tokens, w_in, w_xproj, w_dt, dt_bias, a_log, d_skip, w_out, out_grad):
    tr, tc, model = tokens.shape
    rank, width = w_dt.shape
    states = a_log.shape[0]
    chunks = width // LANES
    pad = -(-tc // 16) * 16
    sizes = (mesh_shape["row"], mesh_shape["col"], tr, tc, chunks, states, rank)
    grid_buf = pltpu.VMEM((chunks, tr * tc, states, LANES), F32)
    row_buf = pltpu.VMEM((chunks, tr, states, LANES), F32)
    col_buf = pltpu.VMEM((chunks, tc, states, LANES), F32)
    wide = pltpu.VMEM((tr, pad, width), F32)
    acc = pltpu.VMEM((tr * pad * states, LANES), F32)
    out = jax.ShapeDtypeStruct((tr, tc, model), BF16)
    return pl.pallas_call(
        functools.partial(layer_kernel, sizes),
        out_shape=(out, out),
        in_specs=[pl.BlockSpec(memory_space=pltpu.VMEM)] * 9,
        out_specs=(pl.BlockSpec(memory_space=pltpu.VMEM),) * 2,
        scratch_shapes=[
            pltpu.VMEM((tr, pad, model), F32)] + [wide] * 11 + [
            pltpu.VMEM((tr, pad, 2 * width), F32), pltpu.VMEM((tr * pad, LANES), F32),
            acc, acc, acc, acc,
            grid_buf, grid_buf, grid_buf, row_buf, col_buf,
            row_buf, col_buf, row_buf, col_buf, row_buf, col_buf, row_buf, col_buf,
            pltpu.VMEM((tc, states, LANES), F32),
            pltpu.SemaphoreType.DMA((4, chunks)),
            pltpu.SemaphoreType.DMA((4, chunks)),
        ],
        compiler_params=pltpu.CompilerParams(
            collective_id=0, has_side_effects=True, vmem_limit_bytes=60 * 1024 * 1024
        ),
    )(
        tokens, w_in, w_xproj, w_dt, dt_bias.reshape(1, width), a_log,
        d_skip.reshape(1, width), w_out, out_grad,
    )


def solution(mesh):
    return jax.shard_map(
        functools.partial(body, dict(mesh.shape)),
        mesh=mesh,
        in_specs=(P("row", "col", None), P(), P(), P(), P(), P(), P(), P(), P("row", "col", None)),
        out_specs=(P("row", "col", None), P("row", "col", None)),
        check_vma=False,
    )
```

```python
import functools
import math

import jax
import jax.numpy as jnp
from jax import lax
from jax.experimental import pallas as pl
from jax.experimental.pallas import tpu as pltpu
from jax.sharding import PartitionSpec as P

MESH = pl.DeviceIdType.MESH
LANES = 128
BLOCK = 256
START, LOCAL, COL_HOP, ROW_HOP, SPACE, NEVER = 1000, 1500, 1500, 3000, 2000, 1 << 30
F32 = jnp.float32
BF16 = jnp.bfloat16


def sigmoid(values):
    return 1.0 / (1.0 + jnp.exp(-values))


def silu_grad(values):
    gate = sigmoid(values)
    return gate * (1.0 + values * (1.0 - gate))


def dot(left, right):
    return jnp.dot(left, right, preferred_element_type=F32)


def dot_transposed(left, right):
    return lax.dot_general(left, right, (((1,), (1,)), ((), ())), preferred_element_type=F32)


def layer_kernel(
    sizes,
    tokens_ref, w_in_ref, w_xproj_ref, w_dt_ref, bias_ref, a_log_ref, skip_ref, w_out_ref, grad_ref,
    layer_ref, token_grad_ref,
    pad_ref, x_pre_ref, z_pre_ref, x_ref, step_ref, u_ref, g_ref, gated_ref, dt_ref,
    out_ref, rb_ref, sd_ref, proj_ref, xd_ref, b_ref, c_ref, bacc_ref, cacc_ref,
    decay, rows, cols, prow, pcol,
    e1r, e1c, e2r, e2c, in1r, in1c, in2r, in2c, fcar,
    send_sem, recv_sem,
):
    n_row, n_col, tr, tc, chunks, states, rank = sizes
    pad = pad_ref.shape[1]
    cells = tr * pad
    width = x_ref.shape[-1]
    model = pad_ref.shape[-1]
    r = lax.axis_index("row")
    p = lax.axis_index("col")
    left, right = (r, lax.rem(p + n_col - 1, n_col)), (r, lax.rem(p + 1, n_col))
    up, down = (lax.rem(r + n_row - 1, n_row), p), (lax.rem(r + 1, n_row), p)
    first_col, last_col = p == 0, p == n_col - 1
    first_row, last_row = r == 0, r == n_row - 1

    barrier = pltpu.get_barrier_semaphore()
    edges = ((first_col, left), (last_col, right), (first_row, up), (last_row, down))
    for edge, neighbour in edges:
        @pl.when(jnp.logical_not(edge))
        def _():
            pl.semaphore_signal(barrier, inc=1, device_id=neighbour, device_id_type=MESH)

    links = (
        (e1r, in1r, right, first_col, last_col, prow),
        (e1c, in1c, up, last_row, first_row, pcol),
        (e2c, in2c, down, first_row, last_row, pcol),
        (e2r, in2r, left, last_col, first_col, prow),
    )

    def copy(kind, k):
        source, target, where = links[kind][:3]
        return pltpu.make_async_remote_copy(
            src_ref=source.at[k],
            dst_ref=target.at[k],
            send_sem=send_sem.at[kind, k],
            recv_sem=recv_sem.at[kind, k],
            device_id=where,
            device_id_type=MESH,
        )

    for kind in range(4):
        @pl.when(links[kind][3])
        def _():
            links[kind][1][...] = jnp.zeros_like(links[kind][1])

    def head_send(kind, k):
        head, tail = links[kind][3:5]

        @pl.when(jnp.logical_and(head, jnp.logical_not(tail)))
        def _():
            copy(kind, k).start()

    def forward(kind, k):
        source, target, _, head, tail, product = links[kind]

        @pl.when(jnp.logical_not(head))
        def _():
            copy(kind, k).wait_recv()

        @pl.when(jnp.logical_not(jnp.logical_or(head, tail)))
        def _():
            source[k] = source[k] + product[k] * target[k]
            copy(kind, k).start()

    def rates(cut):
        return jnp.exp(a_log_ref[:, cut]) * -math.log2(math.e)

    def lanes(k):
        return pl.ds(pl.multiple_of(k * LANES, LANES), LANES)

    def flat(ref):
        return ref[...].reshape(cells, ref.shape[-1])

    def put(ref, cut, values):
        ref[:, :, cut] = values.reshape(tr, pad, values.shape[-1])

    def get(ref, cut):
        values = ref[:, :, cut]
        return values.reshape(cells, values.shape[-1])

    blocks = [slice(at, at + BLOCK) for at in range(0, width, BLOCK)]
    pad_ref[:, tc:, :] = jnp.zeros((tr, pad - tc, model), F32)
    pad_ref[:, :tc, :] = tokens_ref[...].astype(F32)
    tokens = flat(pad_ref).astype(BF16)
    for cut in blocks:
        x_pre = dot(tokens, w_in_ref[:, cut])
        put(x_pre_ref, cut, x_pre)
        put(x_ref, cut, (x_pre * sigmoid(x_pre)).astype(BF16).astype(F32))
    x_dbl = dot_transposed(flat(x_ref).astype(BF16), w_xproj_ref[...])
    xd_ref[:, : rank + 2 * states] = x_dbl
    dt_low = x_dbl[:, :rank].astype(BF16)
    for cut in blocks:
        dt_pre = dot(dt_low, w_dt_ref[:, cut]) + bias_ref[cut].reshape(1, BLOCK)
        step = jnp.maximum(dt_pre, 0.0) + jnp.log1p(jnp.exp(-jnp.abs(dt_pre)))
        put(dt_ref, cut, dt_pre)
        put(step_ref, cut, step)
        put(u_ref, cut, step * get(x_ref, cut))
    pad_ref[:, :tc, :] = grad_ref[...].astype(F32)
    grads = flat(pad_ref).astype(BF16)
    for cut in blocks:
        z_pre = dot(tokens, w_in_ref[:, width + cut.start : width + cut.stop])
        gated = dot_transposed(grads, w_out_ref[cut, :])
        put(z_pre_ref, cut, z_pre)
        put(gated_ref, cut, gated)
        put(g_ref, cut, gated * (z_pre * sigmoid(z_pre)))
    for n in range(states):
        spot = pl.ds(n, cells, stride=states)
        for ref, first in ((b_ref, rank), (c_ref, rank + states)):
            column = xd_ref[:, first + n : first + n + 1]
            ref[spot, :] = jnp.broadcast_to(column, (cells, LANES))

    def cell(i, j):
        return pl.ds(pl.multiple_of((i * pad + j) * states, states), states)

    zero = jnp.zeros((states, LANES), F32)

    bacc_ref[...] = jnp.zeros_like(bacc_ref)
    cacc_ref[...] = jnp.zeros_like(cacc_ref)

    def local_ends(k):
        cut = lanes(k)
        rate = rates(cut)
        csum = jnp.zeros((pad, LANES), F32)
        for i in range(tr):
            steps = step_ref[i, :, cut]
            csum = csum + steps
            prow[k, i] = jnp.exp2(rate * jnp.sum(steps[:tc], axis=0, keepdims=True))
        for j in range(tc):
            pcol[k, j] = jnp.exp2(rate * csum[j : j + 1])

        def line(count, terms):
            i = tr - 1 - count
            state = zero
            after = []
            for j in range(tc):
                t = i * tc + j
                d = jnp.exp2(rate * step_ref[i, j : j + 1, cut])
                decay[k, t] = d
                state = d * state + u_ref[i, j : j + 1, cut] * b_ref[cell(i, j)]
                after.append(d * (terms[j] + g_ref[i, j : j + 1, cut] * c_ref[cell(i, j)]))
            e1r[k, i] = state
            return tuple(after)

        terms = lax.fori_loop(0, tr, line, (zero,) * tc)
        for j in range(tc):
            e1c[k, j] = terms[j]
        head_send(0, k)
        head_send(1, k)

    def row_step(k):
        cut = lanes(k)
        forward(0, k)

        def down_line(i, states_in):
            state = in1r[k, i]
            after = []
            for j in range(tc):
                t = i * tc + j
                d = decay[k, t]
                state = d * state + u_ref[i, j : j + 1, cut] * b_ref[cell(i, j)]
                rows[k, t] = state
                after.append(d * states_in[j] + state)
            return tuple(after)

        ends = lax.fori_loop(0, tr, down_line, (zero,) * tc)
        for j in range(tc):
            e2c[k, j] = ends[j]
        head_send(2, k)

    def col_step(k):
        cut = lanes(k)
        forward(1, k)

        def up_line(count, terms):
            i = tr - 1 - count
            term = zero
            after = [None] * tc
            for j in reversed(range(tc)):
                t = i * tc + j
                d = decay[k, t]
                adjoint = terms[j] + g_ref[i, j : j + 1, cut] * c_ref[cell(i, j)]
                cols[k, t] = adjoint
                after[j] = d * adjoint
                term = d * (adjoint + term)
            e2r[k, i] = term
            return tuple(after)

        lax.fori_loop(0, tr, up_line, tuple(in1c[k, j] for j in range(tc)))
        head_send(3, k)

    def col_link(k):
        forward(2, k)

    def row_link(k):
        forward(3, k)

    def finish(k):
        cut = lanes(k)
        rate = rates(cut)
        for j in range(tc):
            fcar[j] = in2c[k, j]

        def last_line(i, carry):
            term = in2r[k, i]
            for j in reversed(range(tc)):
                t = i * tc + j
                d = decay[k, t]
                adjoint = cols[k, t]
                state = rows[k, t]
                before = in1r[k, i] if j == 0 else rows[k, t - 1]
                passed = d * fcar[j]
                full = passed + state
                fcar[j] = full
                total = adjoint + term
                term = d * total
                slope = adjoint * passed + term * before
                sd_ref[i, j : j + 1, cut] = jnp.sum(slope * rate, axis=0, keepdims=True)
                rb_ref[i, j : j + 1, cut] = jnp.sum(total * b_ref[cell(i, j)], axis=0, keepdims=True)
                out_ref[i, j : j + 1, cut] = jnp.sum(full * c_ref[cell(i, j)], axis=0, keepdims=True)
                bacc_ref[cell(i, j)] += total * u_ref[i, j : j + 1, cut]
                cacc_ref[cell(i, j)] += full * g_ref[i, j : j + 1, cut]
            return carry

        lax.fori_loop(0, tr, last_line, 0)

    below, after = n_row - 1 - r, n_col - 1 - p

    def col_time(k):
        return START + LOCAL + COL_HOP * p + ROW_HOP * r + SPACE * k

    def row_time(k):
        return START + LOCAL + ROW_HOP * below + COL_HOP * after + SPACE * k

    table = (
        (local_ends, lambda k: START * k),
        (row_step, lambda k: START + 1 + COL_HOP * p + START * k),
        (col_step, lambda k: START + 1 + ROW_HOP * below + SPACE * k),
        (col_link, col_time),
        (row_link, row_time),
        (finish, lambda k: jnp.maximum(col_time(k), row_time(k)) + 1),
    )

    def slot(_, counts):
        times = [
            jnp.where(k < chunks, time(k), NEVER) for k, (_, time) in zip(counts, table)
        ]
        best = functools.reduce(jnp.minimum, times)
        free, after_counts = jnp.int32(1), []
        for k, due, (step, _) in zip(counts, times, table):
            hit = jnp.where(due == best, free, 0)
            free = free - hit
            pl.when(hit == 1)(functools.partial(step, k))
            after_counts.append(k + hit)
        return tuple(after_counts)

    peers = sum(jnp.where(edge, 0, 1) for edge, _ in edges)
    pl.semaphore_wait(barrier, peers)
    lax.fori_loop(0, len(table) * chunks, slot, (jnp.int32(0),) * len(table))

    both = jnp.zeros((cells, 2 * states), F32)
    lane = lax.broadcasted_iota(jnp.int32, (LANES, 2 * states), 1)
    for n in range(states):
        spot = pl.ds(n, cells, stride=states)
        for ref, at in ((bacc_ref, n), (cacc_ref, states + n)):
            pick = jnp.where(lane == at, 1.0, 0.0).astype(BF16)
            both = both + dot(ref[spot, :].astype(BF16), pick)
    low_grad = jnp.zeros((cells, rank), F32)
    layer = jnp.zeros((cells, model), F32)
    for cut in blocks:
        x, z_pre, dt_pre = get(x_ref, cut), get(z_pre_ref, cut), get(dt_ref, cut)
        scan_out = get(out_ref, cut) + skip_ref[cut].reshape(1, BLOCK) * x
        layer = layer + dot((scan_out * (z_pre * sigmoid(z_pre))).astype(BF16), w_out_ref[cut, :])
        put(proj_ref, slice(width + cut.start, width + cut.stop),
            get(gated_ref, cut) * scan_out * silu_grad(z_pre))
        step_grad = get(sd_ref, cut) * math.log(2.0) + get(rb_ref, cut) * x
        low_grad = low_grad + dot_transposed(
            (step_grad * sigmoid(dt_pre)).astype(BF16), w_dt_ref[:, cut]
        )
    layer_ref[...] = layer.reshape(tr, pad, model)[:, :tc, :].astype(BF16)
    xd_ref[:, :rank] = low_grad
    xd_ref[:, rank : rank + 2 * states] = both
    dbl_grad = xd_ref[:, : rank + 2 * states].astype(BF16)
    for cut in blocks:
        x_grad = (
            get(rb_ref, cut) * get(step_ref, cut) + get(g_ref, cut) * skip_ref[cut].reshape(1, BLOCK)
            + dot(dbl_grad, w_xproj_ref[:, cut])
        )
        put(proj_ref, cut, x_grad * silu_grad(get(x_pre_ref, cut)))
    proj = flat(proj_ref).astype(BF16)
    for at in range(0, model, BLOCK):
        token_grad = dot_transposed(proj, w_in_ref[at : at + BLOCK, :])
        token_grad_ref[:, :, at : at + BLOCK] = (
            token_grad.reshape(tr, pad, BLOCK)[:, :tc, :].astype(BF16)
        )

    for kind in range(4):
        tail = links[kind][4]

        @pl.when(jnp.logical_not(tail))
        def _():
            @pl.loop(0, chunks)
            def _(k):
                copy(kind, k).wait_send()


def body(mesh_shape, tokens, w_in, w_xproj, w_dt, dt_bias, a_log, d_skip, w_out, out_grad):
    tr, tc, model = tokens.shape
    rank, width = w_dt.shape
    states = a_log.shape[0]
    chunks = width // LANES
    pad = -(-tc // 16) * 16
    sizes = (mesh_shape["row"], mesh_shape["col"], tr, tc, chunks, states, rank)
    grid_buf = pltpu.VMEM((chunks, tr * tc, states, LANES), F32)
    row_buf = pltpu.VMEM((chunks, tr, states, LANES), F32)
    col_buf = pltpu.VMEM((chunks, tc, states, LANES), F32)
    wide = pltpu.VMEM((tr, pad, width), F32)
    acc = pltpu.VMEM((tr * pad * states, LANES), F32)
    out = jax.ShapeDtypeStruct((tr, tc, model), BF16)
    return pl.pallas_call(
        functools.partial(layer_kernel, sizes),
        out_shape=(out, out),
        in_specs=[pl.BlockSpec(memory_space=pltpu.VMEM)] * 9,
        out_specs=(pl.BlockSpec(memory_space=pltpu.VMEM),) * 2,
        scratch_shapes=[
            pltpu.VMEM((tr, pad, model), F32)] + [wide] * 11 + [
            pltpu.VMEM((tr, pad, 2 * width), F32), pltpu.VMEM((tr * pad, LANES), F32),
            acc, acc, acc, acc,
            grid_buf, grid_buf, grid_buf, row_buf, col_buf,
            row_buf, col_buf, row_buf, col_buf, row_buf, col_buf, row_buf, col_buf,
            pltpu.VMEM((tc, states, LANES), F32),
            pltpu.SemaphoreType.DMA((4, chunks)),
            pltpu.SemaphoreType.DMA((4, chunks)),
        ],
        compiler_params=pltpu.CompilerParams(
            collective_id=0, has_side_effects=True, vmem_limit_bytes=60 * 1024 * 1024
        ),
    )(
        tokens, w_in, w_xproj.T, w_dt, dt_bias, a_log, d_skip, w_out, out_grad,
    )


def solution(mesh):
    return jax.shard_map(
        functools.partial(body, dict(mesh.shape)),
        mesh=mesh,
        in_specs=(P("row", "col", None), P(), P(), P(), P(), P(), P(), P(), P("row", "col", None)),
        out_specs=(P("row", "col", None), P("row", "col", None)),
        check_vma=False,
    )
```

```python
import functools
import math

import jax
import jax.numpy as jnp
from jax import lax
from jax.experimental import pallas as pl
from jax.experimental.pallas import tpu as pltpu
from jax.sharding import PartitionSpec as P

MESH = pl.DeviceIdType.MESH
LANES = 128
BLOCK = 256
START, LOCAL, COL_HOP, ROW_HOP, SPACE, NEVER = 1000, 1500, 1500, 3000, 2000, 1 << 30
F32 = jnp.float32
BF16 = jnp.bfloat16


def sigmoid(values):
    return 1.0 / (1.0 + jnp.exp(-values))


def silu_grad(values):
    gate = sigmoid(values)
    return gate * (1.0 + values * (1.0 - gate))


def dot(left, right):
    return jnp.dot(left, right, preferred_element_type=F32)


def dot_transposed(left, right):
    return lax.dot_general(left, right, (((1,), (1,)), ((), ())), preferred_element_type=F32)


def layer_kernel(
    sizes,
    tokens_ref, w_in_ref, w_xproj_ref, w_dt_ref, bias_ref, a_log_ref, skip_ref, w_out_ref, grad_ref,
    layer_ref, token_grad_ref,
    pad_ref, x_pre_ref, z_pre_ref, x_ref, step_ref, u_ref, g_ref, gated_ref, dt_ref,
    out_ref, rb_ref, sd_ref, proj_ref, xd_ref, b_ref, c_ref, bacc_ref, cacc_ref, b_diag, c_diag,
    decay, rows, cols, prow, pcol,
    e1r, e1c, e2r, e2c, in1r, in1c, in2r, in2c, fcar,
    send_sem, recv_sem,
):
    n_row, n_col, tr, tc, chunks, states, rank = sizes
    pad = pad_ref.shape[1]
    cells = tr * pad
    width = x_ref.shape[-1]
    model = pad_ref.shape[-1]
    r = lax.axis_index("row")
    p = lax.axis_index("col")
    left, right = (r, lax.rem(p + n_col - 1, n_col)), (r, lax.rem(p + 1, n_col))
    up, down = (lax.rem(r + n_row - 1, n_row), p), (lax.rem(r + 1, n_row), p)
    first_col, last_col = p == 0, p == n_col - 1
    first_row, last_row = r == 0, r == n_row - 1

    barrier = pltpu.get_barrier_semaphore()
    edges = ((first_col, left), (last_col, right), (first_row, up), (last_row, down))
    for edge, neighbour in edges:
        @pl.when(jnp.logical_not(edge))
        def _():
            pl.semaphore_signal(barrier, inc=1, device_id=neighbour, device_id_type=MESH)

    links = (
        (e1r, in1r, right, first_col, last_col, prow),
        (e1c, in1c, up, last_row, first_row, pcol),
        (e2c, in2c, down, first_row, last_row, pcol),
        (e2r, in2r, left, last_col, first_col, prow),
    )

    def copy(kind, k):
        source, target, where = links[kind][:3]
        return pltpu.make_async_remote_copy(
            src_ref=source.at[k],
            dst_ref=target.at[k],
            send_sem=send_sem.at[kind, k],
            recv_sem=recv_sem.at[kind, k],
            device_id=where,
            device_id_type=MESH,
        )

    for kind in range(4):
        @pl.when(links[kind][3])
        def _():
            links[kind][1][...] = jnp.zeros_like(links[kind][1])

    def head_send(kind, k):
        head, tail = links[kind][3:5]

        @pl.when(jnp.logical_and(head, jnp.logical_not(tail)))
        def _():
            copy(kind, k).start()

    def forward(kind, k):
        source, target, _, head, tail, product = links[kind]

        @pl.when(jnp.logical_not(head))
        def _():
            copy(kind, k).wait_recv()

        @pl.when(jnp.logical_not(jnp.logical_or(head, tail)))
        def _():
            source[k] = source[k] + product[k] * target[k]
            copy(kind, k).start()

    def rates(cut):
        return jnp.exp(a_log_ref[:, cut]) * -math.log2(math.e)

    def lanes(k):
        return pl.ds(pl.multiple_of(k * LANES, LANES), LANES)

    def flat(ref):
        return ref[...].reshape(cells, ref.shape[-1])

    def put(ref, cut, values):
        ref[:, :, cut] = values.reshape(tr, pad, values.shape[-1])

    def get(ref, cut):
        values = ref[:, :, cut]
        return values.reshape(cells, values.shape[-1])

    blocks = [slice(at, at + BLOCK) for at in range(0, width, BLOCK)]
    pad_ref[:, tc:, :] = jnp.zeros((tr, pad - tc, model), F32)
    pad_ref[:, :tc, :] = tokens_ref[...].astype(F32)
    tokens = flat(pad_ref).astype(BF16)
    for cut in blocks:
        x_pre = dot(tokens, w_in_ref[:, cut])
        put(x_pre_ref, cut, x_pre)
        put(x_ref, cut, (x_pre * sigmoid(x_pre)).astype(BF16).astype(F32))
    x_dbl = dot_transposed(flat(x_ref).astype(BF16), w_xproj_ref[...])
    xd_ref[:, : rank + 2 * states] = x_dbl
    dt_low = x_dbl[:, :rank].astype(BF16)
    for cut in blocks:
        dt_pre = dot(dt_low, w_dt_ref[:, cut]) + bias_ref[cut].reshape(1, BLOCK)
        step = jnp.maximum(dt_pre, 0.0) + jnp.log1p(jnp.exp(-jnp.abs(dt_pre)))
        put(dt_ref, cut, dt_pre)
        put(step_ref, cut, step)
        put(u_ref, cut, step * get(x_ref, cut))
    pad_ref[:, :tc, :] = grad_ref[...].astype(F32)
    grads = flat(pad_ref).astype(BF16)
    for cut in blocks:
        z_pre = dot(tokens, w_in_ref[:, width + cut.start : width + cut.stop])
        gated = dot_transposed(grads, w_out_ref[cut, :])
        put(z_pre_ref, cut, z_pre)
        put(gated_ref, cut, gated)
        put(g_ref, cut, gated * (z_pre * sigmoid(z_pre)))
    for n in range(states):
        spot = pl.ds(n, cells, stride=states)
        for ref, first in ((b_ref, rank), (c_ref, rank + states)):
            column = xd_ref[:, first + n : first + n + 1]
            ref[spot, :] = jnp.broadcast_to(column, (cells, LANES))

    place = lax.broadcasted_iota(jnp.int32, (tr, pad, tc * states), 1)
    group = lax.broadcasted_iota(jnp.int32, (tr, pad, tc * states), 2) // states
    on_diag = place == group
    repeat = jnp.where(
        lax.broadcasted_iota(jnp.int32, (states, tc * states), 1) % states
        == lax.broadcasted_iota(jnp.int32, (states, tc * states), 0), 1.0, 0.0
    ).astype(BF16)
    for ref, first in ((b_diag, rank), (c_diag, rank + states)):
        spread = dot(x_dbl[:, first : first + states].astype(BF16), repeat)
        ref[...] = jnp.where(on_diag, spread.reshape(tr, pad, tc * states), 0.0).astype(BF16)
    ones_diag = jnp.where(on_diag[0], 1.0, 0.0).astype(BF16)

    def cell(i, j):
        return pl.ds(pl.multiple_of((i * pad + j) * states, states), states)

    zero = jnp.zeros((states, LANES), F32)

    bacc_ref[...] = jnp.zeros_like(bacc_ref)
    cacc_ref[...] = jnp.zeros_like(cacc_ref)

    def local_ends(k):
        cut = lanes(k)
        rate = rates(cut)
        csum = jnp.zeros((pad, LANES), F32)
        for i in range(tr):
            steps = step_ref[i, :, cut]
            csum = csum + steps
            prow[k, i] = jnp.exp2(rate * jnp.sum(steps[:tc], axis=0, keepdims=True))
        for j in range(tc):
            pcol[k, j] = jnp.exp2(rate * csum[j : j + 1])

        def line(count, terms):
            i = tr - 1 - count
            state = zero
            after = []
            for j in range(tc):
                t = i * tc + j
                d = jnp.exp2(rate * step_ref[i, j : j + 1, cut])
                decay[k, t] = d
                state = d * state + u_ref[i, j : j + 1, cut] * b_ref[cell(i, j)]
                after.append(d * (terms[j] + g_ref[i, j : j + 1, cut] * c_ref[cell(i, j)]))
            e1r[k, i] = state
            return tuple(after)

        terms = lax.fori_loop(0, tr, line, (zero,) * tc)
        for j in range(tc):
            e1c[k, j] = terms[j]
        head_send(0, k)
        head_send(1, k)

    def row_step(k):
        cut = lanes(k)
        forward(0, k)

        def down_line(i, states_in):
            state = in1r[k, i]
            after = []
            for j in range(tc):
                t = i * tc + j
                d = decay[k, t]
                state = d * state + u_ref[i, j : j + 1, cut] * b_ref[cell(i, j)]
                rows[k, t] = state
                after.append(d * states_in[j] + state)
            return tuple(after)

        ends = lax.fori_loop(0, tr, down_line, (zero,) * tc)
        for j in range(tc):
            e2c[k, j] = ends[j]
        head_send(2, k)

    def col_step(k):
        cut = lanes(k)
        forward(1, k)

        def up_line(count, terms):
            i = tr - 1 - count
            term = zero
            after = [None] * tc
            for j in reversed(range(tc)):
                t = i * tc + j
                d = decay[k, t]
                adjoint = terms[j] + g_ref[i, j : j + 1, cut] * c_ref[cell(i, j)]
                cols[k, t] = adjoint
                after[j] = d * adjoint
                term = d * (adjoint + term)
            e2r[k, i] = term
            return tuple(after)

        lax.fori_loop(0, tr, up_line, tuple(in1c[k, j] for j in range(tc)))
        head_send(3, k)

    def col_link(k):
        forward(2, k)

    def row_link(k):
        forward(3, k)

    def finish(k):
        cut = lanes(k)
        rate = rates(cut)
        for j in range(tc):
            fcar[j] = in2c[k, j]

        def last_line(i, carry):
            term = in2r[k, i]
            state = rows[k, i * tc + tc - 1]
            fulls, totals, slopes = [], [], []
            for j in reversed(range(tc)):
                t = i * tc + j
                d = decay[k, t]
                adjoint = cols[k, t]
                before = in1r[k, i] if j == 0 else rows[k, t - 1]
                passed = d * fcar[j]
                full = passed + state
                fcar[j] = full
                total = adjoint + term
                term = d * total
                slope = (adjoint * passed + term * before) * rate
                state = before
                fulls.insert(0, full.astype(BF16))
                totals.insert(0, total.astype(BF16))
                slopes.insert(0, slope.astype(BF16))
            fulls, totals, slopes = (
                jnp.concatenate(parts, axis=0) for parts in (fulls, totals, slopes)
            )
            out_ref[i, :, cut] = dot(c_diag[i], fulls)
            rb_ref[i, :, cut] = dot(b_diag[i], totals)
            sd_ref[i, :, cut] = dot(ones_diag, slopes)
            bacc_ref[i] += dot_transposed(u_ref[i, :, cut].astype(BF16), totals)
            cacc_ref[i] += dot_transposed(g_ref[i, :, cut].astype(BF16), fulls)
            return carry

        lax.fori_loop(0, tr, last_line, 0)

    below, after = n_row - 1 - r, n_col - 1 - p

    def col_time(k):
        return START + LOCAL + COL_HOP * p + ROW_HOP * r + SPACE * k

    def row_time(k):
        return START + LOCAL + ROW_HOP * below + COL_HOP * after + SPACE * k

    table = (
        (local_ends, lambda k: START * k),
        (row_step, lambda k: START + 1 + COL_HOP * p + START * k),
        (col_step, lambda k: START + 1 + ROW_HOP * below + SPACE * k),
        (col_link, col_time),
        (row_link, row_time),
        (finish, lambda k: jnp.maximum(col_time(k), row_time(k)) + 1),
    )

    def slot(_, counts):
        times = [
            jnp.where(k < chunks, time(k), NEVER) for k, (_, time) in zip(counts, table)
        ]
        best = functools.reduce(jnp.minimum, times)
        free, after_counts = jnp.int32(1), []
        for k, due, (step, _) in zip(counts, times, table):
            hit = jnp.where(due == best, free, 0)
            free = free - hit
            pl.when(hit == 1)(functools.partial(step, k))
            after_counts.append(k + hit)
        return tuple(after_counts)

    peers = sum(jnp.where(edge, 0, 1) for edge, _ in edges)
    pl.semaphore_wait(barrier, peers)
    lax.fori_loop(0, len(table) * chunks, slot, (jnp.int32(0),) * len(table))

    both = jnp.zeros((cells, 2 * states), F32)
    spot = lax.broadcasted_iota(jnp.int32, (tc * states, 2 * states), 0) % states
    lane = lax.broadcasted_iota(jnp.int32, (tc * states, 2 * states), 1)
    for ref, first in ((bacc_ref, 0), (cacc_ref, states)):
        pick = jnp.where(lane == spot + first, 1.0, 0.0).astype(BF16)
        kept = jnp.where(on_diag, ref[...], 0.0).reshape(cells, tc * states)
        both = both + dot(kept.astype(BF16), pick)
    low_grad = jnp.zeros((cells, rank), F32)
    layer = jnp.zeros((cells, model), F32)
    for cut in blocks:
        x, z_pre, dt_pre = get(x_ref, cut), get(z_pre_ref, cut), get(dt_ref, cut)
        scan_out = get(out_ref, cut) + skip_ref[cut].reshape(1, BLOCK) * x
        layer = layer + dot((scan_out * (z_pre * sigmoid(z_pre))).astype(BF16), w_out_ref[cut, :])
        put(proj_ref, slice(width + cut.start, width + cut.stop),
            get(gated_ref, cut) * scan_out * silu_grad(z_pre))
        step_grad = get(sd_ref, cut) * math.log(2.0) + get(rb_ref, cut) * x
        low_grad = low_grad + dot_transposed(
            (step_grad * sigmoid(dt_pre)).astype(BF16), w_dt_ref[:, cut]
        )
    layer_ref[...] = layer.reshape(tr, pad, model)[:, :tc, :].astype(BF16)
    xd_ref[:, :rank] = low_grad
    xd_ref[:, rank : rank + 2 * states] = both
    dbl_grad = xd_ref[:, : rank + 2 * states].astype(BF16)
    for cut in blocks:
        x_grad = (
            get(rb_ref, cut) * get(step_ref, cut) + get(g_ref, cut) * skip_ref[cut].reshape(1, BLOCK)
            + dot(dbl_grad, w_xproj_ref[:, cut])
        )
        put(proj_ref, cut, x_grad * silu_grad(get(x_pre_ref, cut)))
    proj = flat(proj_ref).astype(BF16)
    for at in range(0, model, BLOCK):
        token_grad = dot_transposed(proj, w_in_ref[at : at + BLOCK, :])
        token_grad_ref[:, :, at : at + BLOCK] = (
            token_grad.reshape(tr, pad, BLOCK)[:, :tc, :].astype(BF16)
        )

    for kind in range(4):
        tail = links[kind][4]

        @pl.when(jnp.logical_not(tail))
        def _():
            @pl.loop(0, chunks)
            def _(k):
                copy(kind, k).wait_send()


def body(mesh_shape, tokens, w_in, w_xproj, w_dt, dt_bias, a_log, d_skip, w_out, out_grad):
    tr, tc, model = tokens.shape
    rank, width = w_dt.shape
    states = a_log.shape[0]
    chunks = width // LANES
    pad = -(-tc // 16) * 16
    sizes = (mesh_shape["row"], mesh_shape["col"], tr, tc, chunks, states, rank)
    grid_buf = pltpu.VMEM((chunks, tr * tc, states, LANES), F32)
    row_buf = pltpu.VMEM((chunks, tr, states, LANES), F32)
    col_buf = pltpu.VMEM((chunks, tc, states, LANES), F32)
    wide = pltpu.VMEM((tr, pad, width), F32)
    acc = pltpu.VMEM((tr * pad * states, LANES), F32)
    diag = functools.partial(pltpu.VMEM, (tr, pad, tc * states))
    out = jax.ShapeDtypeStruct((tr, tc, model), BF16)
    return pl.pallas_call(
        functools.partial(layer_kernel, sizes),
        out_shape=(out, out),
        in_specs=[pl.BlockSpec(memory_space=pltpu.VMEM)] * 9,
        out_specs=(pl.BlockSpec(memory_space=pltpu.VMEM),) * 2,
        scratch_shapes=[
            pltpu.VMEM((tr, pad, model), F32)] + [wide] * 11 + [
            pltpu.VMEM((tr, pad, 2 * width), F32), pltpu.VMEM((tr * pad, LANES), F32),
            acc, acc, diag(F32), diag(F32), diag(BF16), diag(BF16),
            grid_buf, grid_buf, grid_buf, row_buf, col_buf,
            row_buf, col_buf, row_buf, col_buf, row_buf, col_buf, row_buf, col_buf,
            pltpu.VMEM((tc, states, LANES), F32),
            pltpu.SemaphoreType.DMA((4, chunks)),
            pltpu.SemaphoreType.DMA((4, chunks)),
        ],
        compiler_params=pltpu.CompilerParams(
            collective_id=0, has_side_effects=True, vmem_limit_bytes=60 * 1024 * 1024
        ),
    )(
        tokens, w_in, w_xproj.T, w_dt, dt_bias, a_log, d_skip, w_out, out_grad,
    )


def solution(mesh):
    return jax.shard_map(
        functools.partial(body, dict(mesh.shape)),
        mesh=mesh,
        in_specs=(P("row", "col", None), P(), P(), P(), P(), P(), P(), P(), P("row", "col", None)),
        out_specs=(P("row", "col", None), P("row", "col", None)),
        check_vma=False,
    )
```

```python
import functools
import math

import jax
import jax.numpy as jnp
from jax import lax
from jax.experimental import pallas as pl
from jax.experimental.pallas import tpu as pltpu
from jax.sharding import PartitionSpec as P

MESH = pl.DeviceIdType.MESH
LANES = 128
BLOCK = 256
START, LOCAL, COL_HOP, ROW_HOP, SPACE, NEVER = 1000, 1500, 2500, 3000, 2000, 1 << 30
F32 = jnp.float32
BF16 = jnp.bfloat16


def sigmoid(values):
    return 1.0 / (1.0 + jnp.exp(-values))


def silu_grad(values):
    gate = sigmoid(values)
    return gate * (1.0 + values * (1.0 - gate))


def dot(left, right):
    return jnp.dot(left, right, preferred_element_type=F32)


def dot_transposed(left, right):
    return lax.dot_general(left, right, (((1,), (1,)), ((), ())), preferred_element_type=F32)


def layer_kernel(
    sizes,
    tokens_ref, w_in_ref, w_xproj_ref, w_dt_ref, bias_ref, a_log_ref, skip_ref, w_out_ref, grad_ref,
    layer_ref, token_grad_ref,
    pad_ref, x_pre_ref, z_pre_ref, x_ref, step_ref, u_ref, g_ref, gated_ref, dt_ref,
    out_ref, rb_ref, sd_ref, proj_ref, xd_ref, b_ref, c_ref, bacc_ref, cacc_ref,
    decay, rows, cols, prow, pcol, mate_prow, mate_pcol,
    e1r, e1c, e2r, e2c, in1r, in1c, in2r, in2c, s1r, s1c, s2r, s2c, o1r, o1c, o2r, o2c, fcar,
    rsum, csum, mate_rsum, mate_csum,
    send_sem, recv_sem, swap_send, swap_recv, sum_send, sum_recv,
):
    n_row, n_col, tr, tc, chunks, states, rank = sizes
    pad = pad_ref.shape[1]
    cells = tr * pad
    width = x_ref.shape[-1]
    model = pad_ref.shape[-1]
    r = lax.axis_index("row")
    p = lax.axis_index("col")
    col_mate, row_mate = (r, p + 1 - 2 * (p % 2)), (r + 1 - 2 * (r % 2), p)
    right, left = (r, (p + 2) % n_col), (r, (p + n_col - 2) % n_col)
    down, up = ((r + 2) % n_row, p), ((r + n_row - 2) % n_row, p)
    first_col, last_col = p // 2 == 0, p // 2 == n_col // 2 - 1
    first_row, last_row = r // 2 == 0, r // 2 == n_row // 2 - 1

    barrier = pltpu.get_barrier_semaphore()
    edges = ((first_col, left), (last_col, right), (first_row, up), (last_row, down))
    for mate in (col_mate, row_mate):
        pl.semaphore_signal(barrier, inc=1, device_id=mate, device_id_type=MESH)
    for edge, neighbour in edges:
        @pl.when(jnp.logical_not(edge))
        def _():
            pl.semaphore_signal(barrier, inc=1, device_id=neighbour, device_id_type=MESH)

    links = (
        (e1r, in1r, s1r, o1r, prow, mate_prow, col_mate, right, first_col, last_col, p % 2 == 1),
        (e1c, in1c, s1c, o1c, pcol, mate_pcol, row_mate, up, last_row, first_row, r % 2 == 0),
        (e2c, in2c, s2c, o2c, pcol, mate_pcol, row_mate, down, first_row, last_row, r % 2 == 1),
        (e2r, in2r, s2r, o2r, prow, mate_prow, col_mate, left, last_col, first_col, p % 2 == 0),
    )

    def both(one, other):
        return jnp.logical_and(one, other)

    def swap(kind, k):
        return pltpu.make_async_remote_copy(
            src_ref=links[kind][0].at[k],
            dst_ref=links[kind][1].at[k],
            send_sem=swap_send.at[kind, k],
            recv_sem=swap_recv.at[kind, k],
            device_id=links[kind][6],
            device_id_type=MESH,
        )

    def onward(kind, k):
        return pltpu.make_async_remote_copy(
            src_ref=links[kind][3].at[k],
            dst_ref=links[kind][2].at[k],
            send_sem=send_sem.at[kind, k],
            recv_sem=recv_sem.at[kind, k],
            device_id=links[kind][7],
            device_id_type=MESH,
        )

    def sum_copy(way):
        source, target, mate = ((rsum, mate_rsum, col_mate), (csum, mate_csum, row_mate))[way]
        return pltpu.make_async_remote_copy(
            src_ref=source,
            dst_ref=target,
            send_sem=sum_send.at[way],
            recv_sem=sum_recv.at[way],
            device_id=mate,
            device_id_type=MESH,
        )

    for kind in range(4):
        @pl.when(links[kind][8])
        def _():
            links[kind][2][...] = jnp.zeros_like(links[kind][2])

    def head_send(kind, k):
        last, second = links[kind][9:]

        @pl.when(jnp.logical_not(both(last, second)))
        def _():
            swap(kind, k).start()

    def forward(kind, k):
        own, into, enter, leave, here, there = links[kind][:6]
        first, last, second = links[kind][8:]
        prior = jnp.logical_not(second)

        @pl.when(jnp.logical_not(both(last, prior)))
        def _():
            swap(kind, k).wait_recv()

        @pl.when(jnp.logical_not(first))
        def _():
            onward(kind, k).wait_recv()

        @pl.when(both(jnp.logical_not(last), second))
        def _():
            leave[k] = own[k] + here[k] * (into[k] + there[k] * enter[k])
            onward(kind, k).start()

        @pl.when(both(jnp.logical_not(last), prior))
        def _():
            leave[k] = into[k] + there[k] * (own[k] + here[k] * enter[k])
            onward(kind, k).start()

        @pl.when(second)
        def _():
            into[k] = into[k] + there[k] * enter[k]

        @pl.when(prior)
        def _():
            into[k] = enter[k]

    def lanes(k):
        return pl.ds(pl.multiple_of(k * LANES, LANES), LANES)

    def rates(cut):
        return jnp.exp(a_log_ref[:, cut]) * -math.log2(math.e)

    def flat(ref):
        return ref[...].reshape(cells, ref.shape[-1])

    def put(ref, cut, values):
        ref[:, :, cut] = values.reshape(tr, pad, values.shape[-1])

    def get(ref, cut):
        values = ref[:, :, cut]
        return values.reshape(cells, values.shape[-1])

    blocks = [slice(at, at + BLOCK) for at in range(0, width, BLOCK)]
    pad_ref[:, tc:, :] = jnp.zeros((tr, pad - tc, model), F32)
    pad_ref[:, :tc, :] = tokens_ref[...].astype(F32)
    tokens = flat(pad_ref).astype(BF16)
    for cut in blocks:
        x_pre = dot(tokens, w_in_ref[:, cut])
        put(x_pre_ref, cut, x_pre)
        put(x_ref, cut, (x_pre * sigmoid(x_pre)).astype(BF16).astype(F32))
    x_dbl = dot_transposed(flat(x_ref).astype(BF16), w_xproj_ref[...])
    xd_ref[:, : rank + 2 * states] = x_dbl
    dt_low = x_dbl[:, :rank].astype(BF16)
    for cut in blocks:
        dt_pre = dot(dt_low, w_dt_ref[:, cut]) + bias_ref[cut].reshape(1, BLOCK)
        step = jnp.maximum(dt_pre, 0.0) + jnp.log1p(jnp.exp(-jnp.abs(dt_pre)))
        put(dt_ref, cut, dt_pre)
        put(step_ref, cut, step)
        put(u_ref, cut, step * get(x_ref, cut))
    for cut in blocks:
        totals = jnp.zeros((pad, BLOCK), F32)
        for i in range(tr):
            steps = step_ref[i, :, cut]
            totals = totals + steps
            rsum[i : i + 1, cut] = jnp.sum(steps[:tc], axis=0, keepdims=True)
        csum[:, cut] = totals[:tc]
    peers = 2 + sum(jnp.where(edge, 0, 1) for edge, _ in edges)
    pl.semaphore_wait(barrier, peers)
    for way in range(2):
        sum_copy(way).start()
    pad_ref[:, :tc, :] = grad_ref[...].astype(F32)
    grads = flat(pad_ref).astype(BF16)
    for cut in blocks:
        z_pre = dot(tokens, w_in_ref[:, width + cut.start : width + cut.stop])
        gated = dot_transposed(grads, w_out_ref[cut, :])
        put(z_pre_ref, cut, z_pre)
        put(gated_ref, cut, gated)
        put(g_ref, cut, gated * (z_pre * sigmoid(z_pre)))
    for n in range(states):
        spot = pl.ds(n, cells, stride=states)
        for ref, first in ((b_ref, rank), (c_ref, rank + states)):
            column = xd_ref[:, first + n : first + n + 1]
            ref[spot, :] = jnp.broadcast_to(column, (cells, LANES))

    def cell(i, j):
        return pl.ds(pl.multiple_of((i * pad + j) * states, states), states)

    zero = jnp.zeros((states, LANES), F32)

    bacc_ref[...] = jnp.zeros_like(bacc_ref)
    cacc_ref[...] = jnp.zeros_like(cacc_ref)

    def local_ends(k):
        cut = lanes(k)
        rate = rates(cut)
        for i in range(tr):
            prow[k, i] = jnp.exp2(rate * rsum[i : i + 1, cut])
            mate_prow[k, i] = jnp.exp2(rate * mate_rsum[i : i + 1, cut])
        for j in range(tc):
            pcol[k, j] = jnp.exp2(rate * csum[j : j + 1, cut])
            mate_pcol[k, j] = jnp.exp2(rate * mate_csum[j : j + 1, cut])

        def line(count, terms):
            i = tr - 1 - count
            state = zero
            after = []
            for j in range(tc):
                t = i * tc + j
                d = jnp.exp2(rate * step_ref[i, j : j + 1, cut])
                decay[k, t] = d
                state = d * state + u_ref[i, j : j + 1, cut] * b_ref[cell(i, j)]
                after.append(d * (terms[j] + g_ref[i, j : j + 1, cut] * c_ref[cell(i, j)]))
            e1r[k, i] = state
            return tuple(after)

        terms = lax.fori_loop(0, tr, line, (zero,) * tc)
        for j in range(tc):
            e1c[k, j] = terms[j]
        head_send(0, k)
        head_send(1, k)

    def row_step(k):
        cut = lanes(k)
        forward(0, k)

        def down_line(i, states_in):
            state = in1r[k, i]
            after = []
            for j in range(tc):
                t = i * tc + j
                d = decay[k, t]
                state = d * state + u_ref[i, j : j + 1, cut] * b_ref[cell(i, j)]
                rows[k, t] = state
                after.append(d * states_in[j] + state)
            return tuple(after)

        ends = lax.fori_loop(0, tr, down_line, (zero,) * tc)
        for j in range(tc):
            e2c[k, j] = ends[j]
        head_send(2, k)

    def col_step(k):
        cut = lanes(k)
        forward(1, k)

        def up_line(count, terms):
            i = tr - 1 - count
            term = zero
            after = [None] * tc
            for j in reversed(range(tc)):
                t = i * tc + j
                d = decay[k, t]
                adjoint = terms[j] + g_ref[i, j : j + 1, cut] * c_ref[cell(i, j)]
                cols[k, t] = adjoint
                after[j] = d * adjoint
                term = d * (adjoint + term)
            e2r[k, i] = term
            return tuple(after)

        lax.fori_loop(0, tr, up_line, tuple(in1c[k, j] for j in range(tc)))
        head_send(3, k)

    def col_link(k):
        forward(2, k)

    def row_link(k):
        forward(3, k)

    def finish(k):
        cut = lanes(k)
        rate = rates(cut)
        for j in range(tc):
            fcar[j] = in2c[k, j]

        def last_line(i, carry):
            term = in2r[k, i]
            for j in reversed(range(tc)):
                t = i * tc + j
                d = decay[k, t]
                adjoint = cols[k, t]
                state = rows[k, t]
                before = in1r[k, i] if j == 0 else rows[k, t - 1]
                passed = d * fcar[j]
                full = passed + state
                fcar[j] = full
                total = adjoint + term
                term = d * total
                slope = adjoint * passed + term * before
                sd_ref[i, j : j + 1, cut] = jnp.sum(slope * rate, axis=0, keepdims=True)
                rb_ref[i, j : j + 1, cut] = jnp.sum(total * b_ref[cell(i, j)], axis=0, keepdims=True)
                out_ref[i, j : j + 1, cut] = jnp.sum(full * c_ref[cell(i, j)], axis=0, keepdims=True)
                bacc_ref[cell(i, j)] += total * u_ref[i, j : j + 1, cut]
                cacc_ref[cell(i, j)] += full * g_ref[i, j : j + 1, cut]
            return carry

        lax.fori_loop(0, tr, last_line, 0)

    below, after = (n_row - 1 - r) // 2, (n_col - 1 - p) // 2

    def col_time(k):
        return START + LOCAL + COL_HOP * (p // 2) + ROW_HOP * (r // 2) + SPACE * k

    def row_time(k):
        return START + LOCAL + ROW_HOP * below + COL_HOP * after + SPACE * k

    table = (
        (local_ends, lambda k: START * k),
        (row_step, lambda k: START + 1 + COL_HOP * (p // 2) + START * k),
        (col_step, lambda k: START + 1 + ROW_HOP * below + SPACE * k),
        (col_link, col_time),
        (row_link, row_time),
        (finish, lambda k: jnp.maximum(col_time(k), row_time(k)) + 1),
    )

    def slot(_, counts):
        times = [
            jnp.where(k < chunks, time(k), NEVER) for k, (_, time) in zip(counts, table)
        ]
        best = functools.reduce(jnp.minimum, times)
        free, after_counts = jnp.int32(1), []
        for k, due, (step, _) in zip(counts, times, table):
            hit = jnp.where(due == best, free, 0)
            free = free - hit
            pl.when(hit == 1)(functools.partial(step, k))
            after_counts.append(k + hit)
        return tuple(after_counts)

    for way in range(2):
        sum_copy(way).wait_recv()
    lax.fori_loop(0, len(table) * chunks, slot, (jnp.int32(0),) * len(table))

    narrow = jnp.zeros((cells, 2 * states), F32)
    lane = lax.broadcasted_iota(jnp.int32, (LANES, 2 * states), 1)
    for n in range(states):
        spot = pl.ds(n, cells, stride=states)
        for ref, at in ((bacc_ref, n), (cacc_ref, states + n)):
            pick = jnp.where(lane == at, 1.0, 0.0).astype(BF16)
            narrow = narrow + dot(ref[spot, :].astype(BF16), pick)
    low_grad = jnp.zeros((cells, rank), F32)
    layer = jnp.zeros((cells, model), F32)
    for cut in blocks:
        x, z_pre, dt_pre = get(x_ref, cut), get(z_pre_ref, cut), get(dt_ref, cut)
        scan_out = get(out_ref, cut) + skip_ref[cut].reshape(1, BLOCK) * x
        layer = layer + dot((scan_out * (z_pre * sigmoid(z_pre))).astype(BF16), w_out_ref[cut, :])
        put(proj_ref, slice(width + cut.start, width + cut.stop),
            get(gated_ref, cut) * scan_out * silu_grad(z_pre))
        step_grad = get(sd_ref, cut) * math.log(2.0) + get(rb_ref, cut) * x
        low_grad = low_grad + dot_transposed(
            (step_grad * sigmoid(dt_pre)).astype(BF16), w_dt_ref[:, cut]
        )
    layer_ref[...] = layer.reshape(tr, pad, model)[:, :tc, :].astype(BF16)
    xd_ref[:, :rank] = low_grad
    xd_ref[:, rank : rank + 2 * states] = narrow
    dbl_grad = xd_ref[:, : rank + 2 * states].astype(BF16)
    for cut in blocks:
        x_grad = (
            get(rb_ref, cut) * get(step_ref, cut) + get(g_ref, cut) * skip_ref[cut].reshape(1, BLOCK)
            + dot(dbl_grad, w_xproj_ref[:, cut])
        )
        put(proj_ref, cut, x_grad * silu_grad(get(x_pre_ref, cut)))
    proj = flat(proj_ref).astype(BF16)
    for at in range(0, model, BLOCK):
        token_grad = dot_transposed(proj, w_in_ref[at : at + BLOCK, :])
        token_grad_ref[:, :, at : at + BLOCK] = (
            token_grad.reshape(tr, pad, BLOCK)[:, :tc, :].astype(BF16)
        )

    for way in range(2):
        sum_copy(way).wait_send()
    for kind in range(4):
        last, second = links[kind][9:]

        @pl.when(jnp.logical_not(last))
        def _():
            @pl.loop(0, chunks)
            def _(k):
                onward(kind, k).wait_send()

        @pl.when(jnp.logical_not(both(last, second)))
        def _():
            @pl.loop(0, chunks)
            def _(k):
                swap(kind, k).wait_send()


def body(mesh_shape, tokens, w_in, w_xproj, w_dt, dt_bias, a_log, d_skip, w_out, out_grad):
    tr, tc, model = tokens.shape
    rank, width = w_dt.shape
    states = a_log.shape[0]
    chunks = width // LANES
    pad = -(-tc // 16) * 16
    sizes = (mesh_shape["row"], mesh_shape["col"], tr, tc, chunks, states, rank)
    grid_buf = pltpu.VMEM((chunks, tr * tc, states, LANES), F32)
    row_buf = pltpu.VMEM((chunks, tr, states, LANES), F32)
    col_buf = pltpu.VMEM((chunks, tc, states, LANES), F32)
    wide = pltpu.VMEM((tr, pad, width), F32)
    acc = pltpu.VMEM((tr * pad * states, LANES), F32)
    out = jax.ShapeDtypeStruct((tr, tc, model), BF16)
    return pl.pallas_call(
        functools.partial(layer_kernel, sizes),
        out_shape=(out, out),
        in_specs=[pl.BlockSpec(memory_space=pltpu.VMEM)] * 9,
        out_specs=(pl.BlockSpec(memory_space=pltpu.VMEM),) * 2,
        scratch_shapes=[
            pltpu.VMEM((tr, pad, model), F32)] + [wide] * 11 + [
            pltpu.VMEM((tr, pad, 2 * width), F32), pltpu.VMEM((tr * pad, LANES), F32),
            acc, acc, acc, acc,
            grid_buf, grid_buf, grid_buf, row_buf, col_buf, row_buf, col_buf,
        ] + [row_buf, col_buf, row_buf, col_buf] * 4 + [
            pltpu.VMEM((tc, states, LANES), F32),
            pltpu.VMEM((tr, width), F32), pltpu.VMEM((tc, width), F32),
            pltpu.VMEM((tr, width), F32), pltpu.VMEM((tc, width), F32),
        ] + [pltpu.SemaphoreType.DMA((4, chunks))] * 4 + [pltpu.SemaphoreType.DMA((2,))] * 2 + [
        ],
        compiler_params=pltpu.CompilerParams(
            collective_id=0, has_side_effects=True, vmem_limit_bytes=60 * 1024 * 1024
        ),
    )(
        tokens, w_in, w_xproj.T, w_dt, dt_bias, a_log, d_skip, w_out, out_grad,
    )


def solution(mesh):
    return jax.shard_map(
        functools.partial(body, dict(mesh.shape)),
        mesh=mesh,
        in_specs=(P("row", "col", None), P(), P(), P(), P(), P(), P(), P(), P("row", "col", None)),
        out_specs=(P("row", "col", None), P("row", "col", None)),
        check_vma=False,
    )
```

```python
import functools
import math

import jax
import jax.numpy as jnp
from jax import lax
from jax.experimental import pallas as pl
from jax.experimental.pallas import tpu as pltpu
from jax.sharding import PartitionSpec as P

MESH = pl.DeviceIdType.MESH
LANES = 128
BLOCK = 256
START, LOCAL, COL_HOP, ROW_HOP, SPACE, NEVER = 1000, 1500, 2500, 3000, 2000, 1 << 30
F32 = jnp.float32
BF16 = jnp.bfloat16


def sigmoid(values):
    return 1.0 / (1.0 + jnp.exp(-values))


def silu_grad(values):
    gate = sigmoid(values)
    return gate * (1.0 + values * (1.0 - gate))


def dot(left, right):
    return jnp.dot(left, right, preferred_element_type=F32)


def dot_transposed(left, right):
    return lax.dot_general(left, right, (((1,), (1,)), ((), ())), preferred_element_type=F32)


def layer_kernel(
    sizes,
    tokens_ref, w_in_ref, w_xproj_ref, w_dt_ref, bias_ref, a_log_ref, skip_ref, w_out_ref, grad_ref,
    layer_ref, token_grad_ref,
    pad_ref, x_pre_ref, z_pre_ref, x_ref, step_ref, u_ref, g_ref, gated_ref, dt_ref,
    out_ref, rb_ref, sd_ref, proj_ref, xd_ref, b_ref, c_ref, bacc_ref, cacc_ref,
    decay, rows, cols, prow, pcol, mate_prow, mate_pcol,
    e1r, e1c, e2r, e2c, in1r, in1c, in2r, in2c, s1r, s1c, s2r, s2c, o1r, o1c, o2r, o2c, fcar,
    rsum, csum, mate_rsum, mate_csum,
    send_sem, recv_sem, swap_send, swap_recv, sum_send, sum_recv,
):
    n_row, n_col, tr, tc, chunks, states, rank = sizes
    pad = pad_ref.shape[1]
    cells = tr * pad
    width = x_ref.shape[-1]
    model = pad_ref.shape[-1]
    r = lax.axis_index("row")
    p = lax.axis_index("col")
    col_mate, row_mate = (r, p + 1 - 2 * (p % 2)), (r + 1 - 2 * (r % 2), p)
    right, left = (r, (p + 2) % n_col), (r, (p + n_col - 2) % n_col)
    down, up = ((r + 2) % n_row, p), ((r + n_row - 2) % n_row, p)
    first_col, last_col = p // 2 == 0, p // 2 == n_col // 2 - 1
    first_row, last_row = r // 2 == 0, r // 2 == n_row // 2 - 1

    barrier = pltpu.get_barrier_semaphore()
    edges = ((first_col, left), (last_col, right), (first_row, up), (last_row, down))
    for mate in (col_mate, row_mate):
        pl.semaphore_signal(barrier, inc=1, device_id=mate, device_id_type=MESH)
    for edge, neighbour in edges:
        @pl.when(jnp.logical_not(edge))
        def _():
            pl.semaphore_signal(barrier, inc=1, device_id=neighbour, device_id_type=MESH)

    links = (
        (e1r, in1r, s1r, o1r, prow, mate_prow, col_mate, right, first_col, last_col, p % 2 == 1),
        (e1c, in1c, s1c, o1c, pcol, mate_pcol, row_mate, up, last_row, first_row, r % 2 == 0),
        (e2c, in2c, s2c, o2c, pcol, mate_pcol, row_mate, down, first_row, last_row, r % 2 == 1),
        (e2r, in2r, s2r, o2r, prow, mate_prow, col_mate, left, last_col, first_col, p % 2 == 0),
    )

    def both(one, other):
        return jnp.logical_and(one, other)

    def swap(kind, k):
        return pltpu.make_async_remote_copy(
            src_ref=links[kind][0].at[k],
            dst_ref=links[kind][1].at[k],
            send_sem=swap_send.at[kind, k],
            recv_sem=swap_recv.at[kind, k],
            device_id=links[kind][6],
            device_id_type=MESH,
        )

    def onward(kind, k):
        return pltpu.make_async_remote_copy(
            src_ref=links[kind][3].at[k],
            dst_ref=links[kind][2].at[k],
            send_sem=send_sem.at[kind, k],
            recv_sem=recv_sem.at[kind, k],
            device_id=links[kind][7],
            device_id_type=MESH,
        )

    def sum_copy(way):
        source, target, mate = ((rsum, mate_rsum, col_mate), (csum, mate_csum, row_mate))[way]
        return pltpu.make_async_remote_copy(
            src_ref=source,
            dst_ref=target,
            send_sem=sum_send.at[way],
            recv_sem=sum_recv.at[way],
            device_id=mate,
            device_id_type=MESH,
        )

    for kind in range(4):
        @pl.when(links[kind][8])
        def _():
            links[kind][2][...] = jnp.zeros_like(links[kind][2])

    def head_send(kind, k):
        last, second = links[kind][9:]

        @pl.when(jnp.logical_not(both(last, second)))
        def _():
            swap(kind, k).start()

    def forward(kind, k):
        own, into, enter, leave, here, there = links[kind][:6]
        first, last, second = links[kind][8:]
        prior = jnp.logical_not(second)

        @pl.when(jnp.logical_not(both(last, prior)))
        def _():
            swap(kind, k).wait_recv()

        @pl.when(jnp.logical_not(first))
        def _():
            onward(kind, k).wait_recv()

        @pl.when(both(jnp.logical_not(last), second))
        def _():
            leave[k] = own[k] + here[k] * (into[k] + there[k] * enter[k])
            onward(kind, k).start()

        @pl.when(both(jnp.logical_not(last), prior))
        def _():
            leave[k] = into[k] + there[k] * (own[k] + here[k] * enter[k])
            onward(kind, k).start()

        @pl.when(second)
        def _():
            into[k] = into[k] + there[k] * enter[k]

        @pl.when(prior)
        def _():
            into[k] = enter[k]

    def lanes(k):
        return pl.ds(pl.multiple_of(k * LANES, LANES), LANES)

    def rates(cut):
        return jnp.exp(a_log_ref[:, cut]) * -math.log2(math.e)

    def flat(ref):
        return ref[...].reshape(cells, ref.shape[-1])

    def put(ref, cut, values):
        ref[:, :, cut] = values.reshape(tr, pad, values.shape[-1])

    def get(ref, cut):
        values = ref[:, :, cut]
        return values.reshape(cells, values.shape[-1])

    blocks = [slice(at, at + BLOCK) for at in range(0, width, BLOCK)]
    pad_ref[:, tc:, :] = jnp.zeros((tr, pad - tc, model), F32)
    pad_ref[:, :tc, :] = tokens_ref[...].astype(F32)
    tokens = flat(pad_ref).astype(BF16)
    for cut in blocks:
        x_pre = dot(tokens, w_in_ref[:, cut])
        put(x_pre_ref, cut, x_pre)
        put(x_ref, cut, (x_pre * sigmoid(x_pre)).astype(BF16).astype(F32))
    x_dbl = dot_transposed(flat(x_ref).astype(BF16), w_xproj_ref[...])
    xd_ref[:, : rank + 2 * states] = x_dbl
    dt_low = x_dbl[:, :rank].astype(BF16)
    for cut in blocks:
        dt_pre = dot(dt_low, w_dt_ref[:, cut]) + bias_ref[cut].reshape(1, BLOCK)
        step = jnp.maximum(dt_pre, 0.0) + jnp.log1p(jnp.exp(-jnp.abs(dt_pre)))
        put(dt_ref, cut, dt_pre)
        put(step_ref, cut, step)
        put(u_ref, cut, step * get(x_ref, cut))
    for cut in blocks:
        totals = jnp.zeros((pad, BLOCK), F32)
        for i in range(tr):
            steps = step_ref[i, :, cut]
            totals = totals + steps
            rsum[i : i + 1, cut] = jnp.sum(steps[:tc], axis=0, keepdims=True)
        csum[:, cut] = totals[:tc]
    peers = 2 + sum(jnp.where(edge, 0, 1) for edge, _ in edges)
    pl.semaphore_wait(barrier, peers)
    for way in range(2):
        sum_copy(way).start()
    pad_ref[:, :tc, :] = grad_ref[...].astype(F32)
    grads = flat(pad_ref).astype(BF16)
    for cut in blocks:
        z_pre = dot(tokens, w_in_ref[:, width + cut.start : width + cut.stop])
        gated = dot_transposed(grads, w_out_ref[cut, :])
        put(z_pre_ref, cut, z_pre)
        put(gated_ref, cut, gated)
        put(g_ref, cut, gated * (z_pre * sigmoid(z_pre)))
    for n in range(states):
        spot = pl.ds(n, cells, stride=states)
        for ref, first in ((b_ref, rank), (c_ref, rank + states)):
            column = xd_ref[:, first + n : first + n + 1]
            ref[spot, :] = jnp.broadcast_to(column, (cells, LANES))

    def tile_row(ref, i):
        size = pad * states
        return ref.at[pl.ds(pl.multiple_of(i * size, size), size)]

    def cell(j):
        return slice(j * states, (j + 1) * states)

    zero = jnp.zeros((states, LANES), F32)

    bacc_ref[...] = jnp.zeros_like(bacc_ref)
    cacc_ref[...] = jnp.zeros_like(cacc_ref)

    def local_ends(k):
        cut = lanes(k)
        rate = rates(cut)
        for i in range(tr):
            prow[k, i] = jnp.exp2(rate * rsum[i : i + 1, cut])
            mate_prow[k, i] = jnp.exp2(rate * mate_rsum[i : i + 1, cut])
        for j in range(tc):
            pcol[k, j] = jnp.exp2(rate * csum[j : j + 1, cut])
            mate_pcol[k, j] = jnp.exp2(rate * mate_csum[j : j + 1, cut])

        def line(count, terms):
            i = tr - 1 - count
            b_row, c_row = tile_row(b_ref, i), tile_row(c_ref, i)
            state = zero
            after = []
            for j in range(tc):
                d = jnp.exp2(rate * step_ref[i, j : j + 1, cut])
                decay[k, i, j] = d
                state = d * state + u_ref[i, j : j + 1, cut] * b_row[cell(j)]
                after.append(d * (terms[j] + g_ref[i, j : j + 1, cut] * c_row[cell(j)]))
            e1r[k, i] = state
            return tuple(after)

        terms = lax.fori_loop(0, tr, line, (zero,) * tc, unroll=2)
        for j in range(tc):
            e1c[k, j] = terms[j]
        head_send(0, k)
        head_send(1, k)

    def row_step(k):
        cut = lanes(k)
        forward(0, k)

        def down_line(i, states_in):
            b_row = tile_row(b_ref, i)
            state = in1r[k, i]
            after = []
            for j in range(tc):
                d = decay[k, i, j]
                state = d * state + u_ref[i, j : j + 1, cut] * b_row[cell(j)]
                rows[k, i, j] = state
                after.append(d * states_in[j] + state)
            return tuple(after)

        ends = lax.fori_loop(0, tr, down_line, (zero,) * tc, unroll=2)
        for j in range(tc):
            e2c[k, j] = ends[j]
        head_send(2, k)

    def col_step(k):
        cut = lanes(k)
        forward(1, k)

        def up_line(count, terms):
            i = tr - 1 - count
            c_row = tile_row(c_ref, i)
            term = zero
            after = [None] * tc
            for j in reversed(range(tc)):
                d = decay[k, i, j]
                adjoint = terms[j] + g_ref[i, j : j + 1, cut] * c_row[cell(j)]
                cols[k, i, j] = adjoint
                after[j] = d * adjoint
                term = d * (adjoint + term)
            e2r[k, i] = term
            return tuple(after)

        lax.fori_loop(0, tr, up_line, tuple(in1c[k, j] for j in range(tc)), unroll=2)
        head_send(3, k)

    def col_link(k):
        forward(2, k)

    def row_link(k):
        forward(3, k)

    def finish(k):
        cut = lanes(k)
        rate = rates(cut)
        for j in range(tc):
            fcar[j] = in2c[k, j]

        def last_line(i, carry):
            b_row, c_row = tile_row(b_ref, i), tile_row(c_ref, i)
            bacc_row, cacc_row = tile_row(bacc_ref, i), tile_row(cacc_ref, i)
            term = in2r[k, i]
            state = rows[k, i, tc - 1]
            for j in reversed(range(tc)):
                d = decay[k, i, j]
                adjoint = cols[k, i, j]
                before = in1r[k, i] if j == 0 else rows[k, i, j - 1]
                passed = d * fcar[j]
                full = passed + state
                fcar[j] = full
                total = adjoint + term
                term = d * total
                slope = adjoint * passed + term * before
                state = before
                sd_ref[i, j : j + 1, cut] = jnp.sum(slope * rate, axis=0, keepdims=True)
                rb_ref[i, j : j + 1, cut] = jnp.sum(total * b_row[cell(j)], axis=0, keepdims=True)
                out_ref[i, j : j + 1, cut] = jnp.sum(full * c_row[cell(j)], axis=0, keepdims=True)
                bacc_row[cell(j)] += total * u_ref[i, j : j + 1, cut]
                cacc_row[cell(j)] += full * g_ref[i, j : j + 1, cut]
            return carry

        lax.fori_loop(0, tr, last_line, 0, unroll=2)

    below, after = (n_row - 1 - r) // 2, (n_col - 1 - p) // 2

    def col_time(k):
        return START + LOCAL + COL_HOP * (p // 2) + ROW_HOP * (r // 2) + SPACE * k

    def row_time(k):
        return START + LOCAL + ROW_HOP * below + COL_HOP * after + SPACE * k

    table = (
        (local_ends, lambda k: START * k),
        (row_step, lambda k: START + 1 + COL_HOP * (p // 2) + START * k),
        (col_step, lambda k: START + 1 + ROW_HOP * below + SPACE * k),
        (col_link, col_time),
        (row_link, row_time),
        (finish, lambda k: jnp.maximum(col_time(k), row_time(k)) + 1),
    )

    def slot(_, counts):
        times = [
            jnp.where(k < chunks, time(k), NEVER) for k, (_, time) in zip(counts, table)
        ]
        best = functools.reduce(jnp.minimum, times)
        free, after_counts = jnp.int32(1), []
        for k, due, (step, _) in zip(counts, times, table):
            hit = jnp.where(due == best, free, 0)
            free = free - hit
            pl.when(hit == 1)(functools.partial(step, k))
            after_counts.append(k + hit)
        return tuple(after_counts)

    for way in range(2):
        sum_copy(way).wait_recv()
    lax.fori_loop(0, len(table) * chunks, slot, (jnp.int32(0),) * len(table))

    narrow = jnp.zeros((cells, 2 * states), F32)
    lane = lax.broadcasted_iota(jnp.int32, (LANES, 2 * states), 1)
    for n in range(states):
        spot = pl.ds(n, cells, stride=states)
        for ref, at in ((bacc_ref, n), (cacc_ref, states + n)):
            pick = jnp.where(lane == at, 1.0, 0.0).astype(BF16)
            narrow = narrow + dot(ref[spot, :].astype(BF16), pick)
    low_grad = jnp.zeros((cells, rank), F32)
    layer = jnp.zeros((cells, model), F32)
    for cut in blocks:
        x, z_pre, dt_pre = get(x_ref, cut), get(z_pre_ref, cut), get(dt_ref, cut)
        scan_out = get(out_ref, cut) + skip_ref[cut].reshape(1, BLOCK) * x
        layer = layer + dot((scan_out * (z_pre * sigmoid(z_pre))).astype(BF16), w_out_ref[cut, :])
        put(proj_ref, slice(width + cut.start, width + cut.stop),
            get(gated_ref, cut) * scan_out * silu_grad(z_pre))
        step_grad = get(sd_ref, cut) * math.log(2.0) + get(rb_ref, cut) * x
        low_grad = low_grad + dot_transposed(
            (step_grad * sigmoid(dt_pre)).astype(BF16), w_dt_ref[:, cut]
        )
    layer_ref[...] = layer.reshape(tr, pad, model)[:, :tc, :].astype(BF16)
    xd_ref[:, :rank] = low_grad
    xd_ref[:, rank : rank + 2 * states] = narrow
    dbl_grad = xd_ref[:, : rank + 2 * states].astype(BF16)
    for cut in blocks:
        x_grad = (
            get(rb_ref, cut) * get(step_ref, cut) + get(g_ref, cut) * skip_ref[cut].reshape(1, BLOCK)
            + dot(dbl_grad, w_xproj_ref[:, cut])
        )
        put(proj_ref, cut, x_grad * silu_grad(get(x_pre_ref, cut)))
    proj = flat(proj_ref).astype(BF16)
    for at in range(0, model, BLOCK):
        token_grad = dot_transposed(proj, w_in_ref[at : at + BLOCK, :])
        token_grad_ref[:, :, at : at + BLOCK] = (
            token_grad.reshape(tr, pad, BLOCK)[:, :tc, :].astype(BF16)
        )

    for way in range(2):
        sum_copy(way).wait_send()
    for kind in range(4):
        last, second = links[kind][9:]

        @pl.when(jnp.logical_not(last))
        def _():
            @pl.loop(0, chunks)
            def _(k):
                onward(kind, k).wait_send()

        @pl.when(jnp.logical_not(both(last, second)))
        def _():
            @pl.loop(0, chunks)
            def _(k):
                swap(kind, k).wait_send()


def body(mesh_shape, tokens, w_in, w_xproj, w_dt, dt_bias, a_log, d_skip, w_out, out_grad):
    tr, tc, model = tokens.shape
    rank, width = w_dt.shape
    states = a_log.shape[0]
    chunks = width // LANES
    pad = -(-tc // 16) * 16
    sizes = (mesh_shape["row"], mesh_shape["col"], tr, tc, chunks, states, rank)
    grid_buf = pltpu.VMEM((chunks, tr, tc, states, LANES), F32)
    row_buf = pltpu.VMEM((chunks, tr, states, LANES), F32)
    col_buf = pltpu.VMEM((chunks, tc, states, LANES), F32)
    wide = pltpu.VMEM((tr, pad, width), F32)
    acc = pltpu.VMEM((tr * pad * states, LANES), F32)
    out = jax.ShapeDtypeStruct((tr, tc, model), BF16)
    return pl.pallas_call(
        functools.partial(layer_kernel, sizes),
        out_shape=(out, out),
        in_specs=[pl.BlockSpec(memory_space=pltpu.VMEM)] * 9,
        out_specs=(pl.BlockSpec(memory_space=pltpu.VMEM),) * 2,
        scratch_shapes=[
            pltpu.VMEM((tr, pad, model), F32)] + [wide] * 11 + [
            pltpu.VMEM((tr, pad, 2 * width), F32), pltpu.VMEM((tr * pad, LANES), F32),
            acc, acc, acc, acc,
            grid_buf, grid_buf, grid_buf, row_buf, col_buf, row_buf, col_buf,
        ] + [row_buf, col_buf, row_buf, col_buf] * 4 + [
            pltpu.VMEM((tc, states, LANES), F32),
            pltpu.VMEM((tr, width), F32), pltpu.VMEM((tc, width), F32),
            pltpu.VMEM((tr, width), F32), pltpu.VMEM((tc, width), F32),
        ] + [pltpu.SemaphoreType.DMA((4, chunks))] * 4 + [pltpu.SemaphoreType.DMA((2,))] * 2 + [
        ],
        compiler_params=pltpu.CompilerParams(
            collective_id=0, has_side_effects=True, vmem_limit_bytes=60 * 1024 * 1024
        ),
    )(
        tokens, w_in, w_xproj.T, w_dt, dt_bias, a_log, d_skip, w_out, out_grad,
    )


def solution(mesh):
    return jax.shard_map(
        functools.partial(body, dict(mesh.shape)),
        mesh=mesh,
        in_specs=(P("row", "col", None), P(), P(), P(), P(), P(), P(), P(), P("row", "col", None)),
        out_specs=(P("row", "col", None), P("row", "col", None)),
        check_vma=False,
    )
```

```python
import functools
import math

import jax
import jax.numpy as jnp
from jax import lax
from jax.experimental import pallas as pl
from jax.experimental.pallas import tpu as pltpu
from jax.sharding import PartitionSpec as P

MESH = pl.DeviceIdType.MESH
LANES = 128
BLOCK = 256
START, LOCAL, COL_HOP, ROW_HOP, SPACE, LATER, NEVER = 1000, 1500, 2500, 3000, 2000, 4000, 1 << 30
F32 = jnp.float32
BF16 = jnp.bfloat16


def sigmoid(values):
    return 1.0 / (1.0 + jnp.exp(-values))


def silu_grad(values):
    gate = sigmoid(values)
    return gate * (1.0 + values * (1.0 - gate))


def dot(left, right):
    return jnp.dot(left, right, preferred_element_type=F32)


def dot_transposed(left, right):
    return lax.dot_general(left, right, (((1,), (1,)), ((), ())), preferred_element_type=F32)


def layer_kernel(
    sizes,
    tokens_ref, w_in_ref, w_xproj_ref, w_dt_ref, bias_ref, a_log_ref, skip_ref, w_out_ref, grad_ref,
    layer_ref, token_grad_ref,
    pad_ref, x_pre_ref, z_pre_ref, x_ref, step_ref, u_ref, g_ref, gated_ref, dt_ref,
    out_ref, rb_ref, sd_ref, proj_ref, xd_ref, b_ref, c_ref, bacc_ref, cacc_ref,
    decay, rows, cols, prow, pcol, mate_prow, mate_pcol,
    e1r, e1c, e2r, e2c, in1r, in1c, in2r, in2c, s1r, s1c, s2r, s2c, o1r, o1c, o2r, o2c, fcar,
    rsum, csum, mate_rsum, mate_csum,
    send_sem, recv_sem, swap_send, swap_recv, sum_send, sum_recv,
):
    n_row, n_col, tr, tc, chunks, states, rank = sizes
    pad = pad_ref.shape[1]
    cells = tr * pad
    width = x_ref.shape[-1]
    model = pad_ref.shape[-1]
    r = lax.axis_index("row")
    p = lax.axis_index("col")
    col_mate, row_mate = (r, p + 1 - 2 * (p % 2)), (r + 1 - 2 * (r % 2), p)
    right, left = (r, (p + 2) % n_col), (r, (p + n_col - 2) % n_col)
    down, up = ((r + 2) % n_row, p), ((r + n_row - 2) % n_row, p)
    first_col, last_col = p // 2 == 0, p // 2 == n_col // 2 - 1
    first_row, last_row = r // 2 == 0, r // 2 == n_row // 2 - 1

    barrier = pltpu.get_barrier_semaphore()
    edges = ((first_col, left), (last_col, right), (first_row, up), (last_row, down))
    for mate in (col_mate, row_mate):
        pl.semaphore_signal(barrier, inc=1, device_id=mate, device_id_type=MESH)
    for edge, neighbour in edges:
        @pl.when(jnp.logical_not(edge))
        def _():
            pl.semaphore_signal(barrier, inc=1, device_id=neighbour, device_id_type=MESH)

    links = (
        (e1r, in1r, s1r, o1r, prow, mate_prow, col_mate, right, first_col, last_col, p % 2 == 1),
        (e1c, in1c, s1c, o1c, pcol, mate_pcol, row_mate, up, last_row, first_row, r % 2 == 0),
        (e2c, in2c, s2c, o2c, pcol, mate_pcol, row_mate, down, first_row, last_row, r % 2 == 1),
        (e2r, in2r, s2r, o2r, prow, mate_prow, col_mate, left, last_col, first_col, p % 2 == 0),
    )

    def both(one, other):
        return jnp.logical_and(one, other)

    def swap(kind, k):
        return pltpu.make_async_remote_copy(
            src_ref=links[kind][0].at[k],
            dst_ref=links[kind][1].at[k],
            send_sem=swap_send.at[kind, k],
            recv_sem=swap_recv.at[kind, k],
            device_id=links[kind][6],
            device_id_type=MESH,
        )

    def onward(kind, k):
        return pltpu.make_async_remote_copy(
            src_ref=links[kind][3].at[k],
            dst_ref=links[kind][2].at[k],
            send_sem=send_sem.at[kind, k],
            recv_sem=recv_sem.at[kind, k],
            device_id=links[kind][7],
            device_id_type=MESH,
        )

    def sum_copy(way):
        source, target, mate = ((rsum, mate_rsum, col_mate), (csum, mate_csum, row_mate))[way]
        return pltpu.make_async_remote_copy(
            src_ref=source,
            dst_ref=target,
            send_sem=sum_send.at[way],
            recv_sem=sum_recv.at[way],
            device_id=mate,
            device_id_type=MESH,
        )

    for kind in range(4):
        @pl.when(links[kind][8])
        def _():
            links[kind][2][...] = jnp.zeros_like(links[kind][2])

    def head_send(kind, k):
        last, second = links[kind][9:]

        @pl.when(jnp.logical_not(both(last, second)))
        def _():
            swap(kind, k).start()

    def forward(kind, k):
        own, into, enter, leave, here, there = links[kind][:6]
        first, last, second = links[kind][8:]
        prior = jnp.logical_not(second)

        @pl.when(jnp.logical_not(both(last, prior)))
        def _():
            swap(kind, k).wait_recv()

        @pl.when(jnp.logical_not(first))
        def _():
            onward(kind, k).wait_recv()

        @pl.when(both(jnp.logical_not(last), second))
        def _():
            leave[k] = own[k] + here[k] * (into[k] + there[k] * enter[k])
            onward(kind, k).start()

        @pl.when(both(jnp.logical_not(last), prior))
        def _():
            leave[k] = into[k] + there[k] * (own[k] + here[k] * enter[k])
            onward(kind, k).start()

        @pl.when(second)
        def _():
            into[k] = into[k] + there[k] * enter[k]

        @pl.when(prior)
        def _():
            into[k] = enter[k]

    def lanes(k):
        return pl.ds(pl.multiple_of(k * LANES, LANES), LANES)

    def rates(cut):
        return jnp.exp(a_log_ref[:, cut]) * -math.log2(math.e)

    def flat(ref):
        return ref[...].reshape(cells, ref.shape[-1])

    def put(ref, cut, values):
        ref[:, :, cut] = values.reshape(tr, pad, values.shape[-1])

    def get(ref, cut):
        values = ref[:, :, cut]
        return values.reshape(cells, values.shape[-1])

    blocks = [slice(at, at + BLOCK) for at in range(0, width, BLOCK)]
    pad_ref[:, tc:, :] = jnp.zeros((tr, pad - tc, model), F32)
    pad_ref[:, :tc, :] = tokens_ref[...].astype(F32)
    tokens = flat(pad_ref).astype(BF16)
    for cut in blocks:
        x_pre = dot(tokens, w_in_ref[:, cut])
        put(x_pre_ref, cut, x_pre)
        put(x_ref, cut, (x_pre * sigmoid(x_pre)).astype(BF16).astype(F32))
    x_dbl = dot_transposed(flat(x_ref).astype(BF16), w_xproj_ref[...])
    xd_ref[:, : rank + 2 * states] = x_dbl
    dt_low = x_dbl[:, :rank].astype(BF16)
    for cut in blocks:
        dt_pre = dot(dt_low, w_dt_ref[:, cut]) + bias_ref[cut].reshape(1, BLOCK)
        step = jnp.maximum(dt_pre, 0.0) + jnp.log1p(jnp.exp(-jnp.abs(dt_pre)))
        put(dt_ref, cut, dt_pre)
        put(step_ref, cut, step)
        put(u_ref, cut, step * get(x_ref, cut))
    for cut in blocks:
        totals = jnp.zeros((pad, BLOCK), F32)
        for i in range(tr):
            steps = step_ref[i, :, cut]
            totals = totals + steps
            rsum[i : i + 1, cut] = jnp.sum(steps[:tc], axis=0, keepdims=True)
        csum[:, cut] = totals[:tc]
    peers = 2 + sum(jnp.where(edge, 0, 1) for edge, _ in edges)
    pl.semaphore_wait(barrier, peers)
    for way in range(2):
        sum_copy(way).start()
    pad_ref[:, :tc, :] = grad_ref[...].astype(F32)
    grads = flat(pad_ref).astype(BF16)
    for cut in blocks:
        z_pre = dot(tokens, w_in_ref[:, width + cut.start : width + cut.stop])
        gated = dot_transposed(grads, w_out_ref[cut, :])
        put(z_pre_ref, cut, z_pre)
        put(gated_ref, cut, gated)
        put(g_ref, cut, gated * (z_pre * sigmoid(z_pre)))
    for n in range(states):
        spot = pl.ds(n, cells, stride=states)
        for ref, first in ((b_ref, rank), (c_ref, rank + states)):
            column = xd_ref[:, first + n : first + n + 1]
            ref[spot, :] = jnp.broadcast_to(column, (cells, LANES))

    def tile_row(ref, i):
        size = pad * states
        return ref.at[pl.ds(pl.multiple_of(i * size, size), size)]

    def cell(j):
        return slice(j * states, (j + 1) * states)

    zero = jnp.zeros((states, LANES), F32)

    bacc_ref[...] = jnp.zeros_like(bacc_ref)
    cacc_ref[...] = jnp.zeros_like(cacc_ref)

    def local_ends(k):
        cut = lanes(k)
        rate = rates(cut)
        for i in range(tr):
            prow[k, i] = jnp.exp2(rate * rsum[i : i + 1, cut])
            mate_prow[k, i] = jnp.exp2(rate * mate_rsum[i : i + 1, cut])
        for j in range(tc):
            pcol[k, j] = jnp.exp2(rate * csum[j : j + 1, cut])
            mate_pcol[k, j] = jnp.exp2(rate * mate_csum[j : j + 1, cut])

        def line(count, terms):
            i = tr - 1 - count
            b_row, c_row = tile_row(b_ref, i), tile_row(c_ref, i)
            state = zero
            after = []
            for j in range(tc):
                d = jnp.exp2(rate * step_ref[i, j : j + 1, cut])
                decay[k, i, j] = d
                state = d * state + u_ref[i, j : j + 1, cut] * b_row[cell(j)]
                after.append(d * (terms[j] + g_ref[i, j : j + 1, cut] * c_row[cell(j)]))
            e1r[k, i] = state
            return tuple(after)

        terms = lax.fori_loop(0, tr, line, (zero,) * tc)
        for j in range(tc):
            e1c[k, j] = terms[j]
        head_send(0, k)
        head_send(1, k)

    def row_step(k):
        cut = lanes(k)
        forward(0, k)

        def down_line(i, states_in):
            b_row = tile_row(b_ref, i)
            state = in1r[k, i]
            after = []
            for j in range(tc):
                d = decay[k, i, j]
                state = d * state + u_ref[i, j : j + 1, cut] * b_row[cell(j)]
                rows[k, i, j] = state
                after.append(d * states_in[j] + state)
            return tuple(after)

        ends = lax.fori_loop(0, tr, down_line, (zero,) * tc)
        for j in range(tc):
            e2c[k, j] = ends[j]
        head_send(2, k)

    def col_step(k):
        cut = lanes(k)
        forward(1, k)

        def up_line(count, terms):
            i = tr - 1 - count
            c_row = tile_row(c_ref, i)
            term = zero
            after = [None] * tc
            for j in reversed(range(tc)):
                d = decay[k, i, j]
                adjoint = terms[j] + g_ref[i, j : j + 1, cut] * c_row[cell(j)]
                cols[k, i, j] = adjoint
                after[j] = d * adjoint
                term = d * (adjoint + term)
            e2r[k, i] = term
            return tuple(after)

        lax.fori_loop(0, tr, up_line, tuple(in1c[k, j] for j in range(tc)))
        head_send(3, k)

    def col_link(k):
        forward(2, k)

    def row_link(k):
        forward(3, k)

    def finish(k):
        cut = lanes(k)
        rate = rates(cut)
        for j in range(tc):
            fcar[j] = in2c[k, j]

        def last_line(i, carry):
            b_row, c_row = tile_row(b_ref, i), tile_row(c_ref, i)
            bacc_row, cacc_row = tile_row(bacc_ref, i), tile_row(cacc_ref, i)
            term = in2r[k, i]
            state = rows[k, i, tc - 1]
            for j in reversed(range(tc)):
                d = decay[k, i, j]
                adjoint = cols[k, i, j]
                before = in1r[k, i] if j == 0 else rows[k, i, j - 1]
                passed = d * fcar[j]
                full = passed + state
                fcar[j] = full
                total = adjoint + term
                term = d * total
                slope = adjoint * passed + term * before
                state = before
                sd_ref[i, j : j + 1, cut] = jnp.sum(slope * rate, axis=0, keepdims=True)
                rb_ref[i, j : j + 1, cut] = jnp.sum(total * b_row[cell(j)], axis=0, keepdims=True)
                out_ref[i, j : j + 1, cut] = jnp.sum(full * c_row[cell(j)], axis=0, keepdims=True)
                bacc_row[cell(j)] += total * u_ref[i, j : j + 1, cut]
                cacc_row[cell(j)] += full * g_ref[i, j : j + 1, cut]
            return carry

        lax.fori_loop(0, tr, last_line, 0)

    below, after = (n_row - 1 - r) // 2, (n_col - 1 - p) // 2

    def col_time(k):
        return START + LOCAL + COL_HOP * (p // 2) + ROW_HOP * (r // 2) + SPACE * k

    def row_time(k):
        return START + LOCAL + ROW_HOP * below + COL_HOP * after + SPACE * k

    table = (
        (local_ends, lambda k: START * k),
        (row_step, lambda k: START + 1 + COL_HOP * (p // 2) + START * k),
        (col_step, lambda k: START + 1 + ROW_HOP * below + START * k),
        (col_link, col_time),
        (row_link, row_time),
        (finish, lambda k: 1 + jnp.maximum(
            col_time(k) + jnp.where(last_row, 0, LATER), row_time(k) + jnp.where(first_col, 0, LATER)
        )),
    )

    def slot(_, counts):
        times = [
            jnp.where(k < chunks, time(k), NEVER) for k, (_, time) in zip(counts, table)
        ]
        best = functools.reduce(jnp.minimum, times)
        free, after_counts = jnp.int32(1), []
        for k, due, (step, _) in zip(counts, times, table):
            hit = jnp.where(due == best, free, 0)
            free = free - hit
            pl.when(hit == 1)(functools.partial(step, k))
            after_counts.append(k + hit)
        return tuple(after_counts)

    for way in range(2):
        sum_copy(way).wait_recv()
    lax.fori_loop(0, len(table) * chunks, slot, (jnp.int32(0),) * len(table))

    narrow = jnp.zeros((cells, 2 * states), F32)
    lane = lax.broadcasted_iota(jnp.int32, (LANES, 2 * states), 1)
    for n in range(states):
        spot = pl.ds(n, cells, stride=states)
        for ref, at in ((bacc_ref, n), (cacc_ref, states + n)):
            pick = jnp.where(lane == at, 1.0, 0.0).astype(BF16)
            narrow = narrow + dot(ref[spot, :].astype(BF16), pick)
    low_grad = jnp.zeros((cells, rank), F32)
    layer = jnp.zeros((cells, model), F32)
    for cut in blocks:
        x, z_pre, dt_pre = get(x_ref, cut), get(z_pre_ref, cut), get(dt_ref, cut)
        scan_out = get(out_ref, cut) + skip_ref[cut].reshape(1, BLOCK) * x
        layer = layer + dot((scan_out * (z_pre * sigmoid(z_pre))).astype(BF16), w_out_ref[cut, :])
        put(proj_ref, slice(width + cut.start, width + cut.stop),
            get(gated_ref, cut) * scan_out * silu_grad(z_pre))
        step_grad = get(sd_ref, cut) * math.log(2.0) + get(rb_ref, cut) * x
        low_grad = low_grad + dot_transposed(
            (step_grad * sigmoid(dt_pre)).astype(BF16), w_dt_ref[:, cut]
        )
    layer_ref[...] = layer.reshape(tr, pad, model)[:, :tc, :].astype(BF16)
    xd_ref[:, :rank] = low_grad
    xd_ref[:, rank : rank + 2 * states] = narrow
    dbl_grad = xd_ref[:, : rank + 2 * states].astype(BF16)
    for cut in blocks:
        x_grad = (
            get(rb_ref, cut) * get(step_ref, cut) + get(g_ref, cut) * skip_ref[cut].reshape(1, BLOCK)
            + dot(dbl_grad, w_xproj_ref[:, cut])
        )
        put(proj_ref, cut, x_grad * silu_grad(get(x_pre_ref, cut)))
    proj = flat(proj_ref).astype(BF16)
    for at in range(0, model, BLOCK):
        token_grad = dot_transposed(proj, w_in_ref[at : at + BLOCK, :])
        token_grad_ref[:, :, at : at + BLOCK] = (
            token_grad.reshape(tr, pad, BLOCK)[:, :tc, :].astype(BF16)
        )

    for way in range(2):
        sum_copy(way).wait_send()
    for kind in range(4):
        last, second = links[kind][9:]

        @pl.when(jnp.logical_not(last))
        def _():
            @pl.loop(0, chunks)
            def _(k):
                onward(kind, k).wait_send()

        @pl.when(jnp.logical_not(both(last, second)))
        def _():
            @pl.loop(0, chunks)
            def _(k):
                swap(kind, k).wait_send()


def body(mesh_shape, tokens, w_in, w_xproj, w_dt, dt_bias, a_log, d_skip, w_out, out_grad):
    tr, tc, model = tokens.shape
    rank, width = w_dt.shape
    states = a_log.shape[0]
    chunks = width // LANES
    pad = -(-tc // 16) * 16
    sizes = (mesh_shape["row"], mesh_shape["col"], tr, tc, chunks, states, rank)
    grid_buf = pltpu.VMEM((chunks, tr, tc, states, LANES), F32)
    row_buf = pltpu.VMEM((chunks, tr, states, LANES), F32)
    col_buf = pltpu.VMEM((chunks, tc, states, LANES), F32)
    wide = pltpu.VMEM((tr, pad, width), F32)
    acc = pltpu.VMEM((tr * pad * states, LANES), F32)
    out = jax.ShapeDtypeStruct((tr, tc, model), BF16)
    return pl.pallas_call(
        functools.partial(layer_kernel, sizes),
        out_shape=(out, out),
        in_specs=[pl.BlockSpec(memory_space=pltpu.VMEM)] * 9,
        out_specs=(pl.BlockSpec(memory_space=pltpu.VMEM),) * 2,
        scratch_shapes=[
            pltpu.VMEM((tr, pad, model), F32)] + [wide] * 11 + [
            pltpu.VMEM((tr, pad, 2 * width), F32), pltpu.VMEM((tr * pad, LANES), F32),
            acc, acc, acc, acc,
            grid_buf, grid_buf, grid_buf, row_buf, col_buf, row_buf, col_buf,
        ] + [row_buf, col_buf, row_buf, col_buf] * 4 + [
            pltpu.VMEM((tc, states, LANES), F32),
            pltpu.VMEM((tr, width), F32), pltpu.VMEM((tc, width), F32),
            pltpu.VMEM((tr, width), F32), pltpu.VMEM((tc, width), F32),
        ] + [pltpu.SemaphoreType.DMA((4, chunks))] * 4 + [pltpu.SemaphoreType.DMA((2,))] * 2 + [
        ],
        compiler_params=pltpu.CompilerParams(
            collective_id=0, has_side_effects=True, vmem_limit_bytes=60 * 1024 * 1024
        ),
    )(
        tokens, w_in, w_xproj.T, w_dt, dt_bias, a_log, d_skip, w_out, out_grad,
    )


def solution(mesh):
    return jax.shard_map(
        functools.partial(body, dict(mesh.shape)),
        mesh=mesh,
        in_specs=(P("row", "col", None), P(), P(), P(), P(), P(), P(), P(), P("row", "col", None)),
        out_specs=(P("row", "col", None), P("row", "col", None)),
        check_vma=False,
    )
```

```python
import functools
import math

import jax
import jax.numpy as jnp
from jax import lax
from jax.experimental import pallas as pl
from jax.experimental.pallas import tpu as pltpu
from jax.sharding import PartitionSpec as P

MESH = pl.DeviceIdType.MESH
LANES = 128
BLOCK = 256
START, LOCAL, COL_HOP, ROW_HOP, SPACE, NEVER = 1000, 1500, 2500, 3000, 2000, 1 << 30
F32 = jnp.float32
BF16 = jnp.bfloat16


def sigmoid(values):
    return 0.5 + 0.5 * jnp.tanh(0.5 * values)


def silu_grad(values):
    gate = sigmoid(values)
    return gate * (1.0 + values * (1.0 - gate))


def dot(left, right):
    return jnp.dot(left, right, preferred_element_type=F32)


def dot_transposed(left, right):
    return lax.dot_general(left, right, (((1,), (1,)), ((), ())), preferred_element_type=F32)


def layer_kernel(
    sizes,
    tokens_ref, w_in_ref, w_xproj_ref, w_dt_ref, bias_ref, a_log_ref, skip_ref, w_out_ref, grad_ref,
    layer_ref, token_grad_ref,
    pad_ref, x_pre_ref, z_pre_ref, x_ref, step_ref, u_ref, g_ref, gated_ref, dt_ref,
    out_ref, rb_ref, sd_ref, proj_ref, xd_ref, b_ref, c_ref, bacc_ref, cacc_ref,
    decay, rows, cols, prow, pcol, mate_prow, mate_pcol,
    e1r, e1c, e2r, e2c, in1r, in1c, in2r, in2c, s1r, s1c, s2r, s2c, o1r, o1c, o2r, o2c, fcar,
    rsum, csum, mate_rsum, mate_csum,
    send_sem, recv_sem, swap_send, swap_recv, sum_send, sum_recv,
):
    n_row, n_col, tr, tc, chunks, states, rank = sizes
    pad = pad_ref.shape[1]
    cells = tr * pad
    width = x_ref.shape[-1]
    model = pad_ref.shape[-1]
    r = lax.axis_index("row")
    p = lax.axis_index("col")
    col_mate, row_mate = (r, p + 1 - 2 * (p % 2)), (r + 1 - 2 * (r % 2), p)
    right, left = (r, (p + 2) % n_col), (r, (p + n_col - 2) % n_col)
    down, up = ((r + 2) % n_row, p), ((r + n_row - 2) % n_row, p)
    first_col, last_col = p // 2 == 0, p // 2 == n_col // 2 - 1
    first_row, last_row = r // 2 == 0, r // 2 == n_row // 2 - 1

    barrier = pltpu.get_barrier_semaphore()
    edges = ((first_col, left), (last_col, right), (first_row, up), (last_row, down))
    for mate in (col_mate, row_mate):
        pl.semaphore_signal(barrier, inc=1, device_id=mate, device_id_type=MESH)
    for edge, neighbour in edges:
        @pl.when(jnp.logical_not(edge))
        def _():
            pl.semaphore_signal(barrier, inc=1, device_id=neighbour, device_id_type=MESH)

    links = (
        (e1r, in1r, s1r, o1r, prow, mate_prow, col_mate, right, first_col, last_col, p % 2 == 1),
        (e1c, in1c, s1c, o1c, pcol, mate_pcol, row_mate, up, last_row, first_row, r % 2 == 0),
        (e2c, in2c, s2c, o2c, pcol, mate_pcol, row_mate, down, first_row, last_row, r % 2 == 1),
        (e2r, in2r, s2r, o2r, prow, mate_prow, col_mate, left, last_col, first_col, p % 2 == 0),
    )

    def both(one, other):
        return jnp.logical_and(one, other)

    def swap(kind, k):
        return pltpu.make_async_remote_copy(
            src_ref=links[kind][0].at[k],
            dst_ref=links[kind][1].at[k],
            send_sem=swap_send.at[kind, k],
            recv_sem=swap_recv.at[kind, k],
            device_id=links[kind][6],
            device_id_type=MESH,
        )

    def onward(kind, k):
        return pltpu.make_async_remote_copy(
            src_ref=links[kind][3].at[k],
            dst_ref=links[kind][2].at[k],
            send_sem=send_sem.at[kind, k],
            recv_sem=recv_sem.at[kind, k],
            device_id=links[kind][7],
            device_id_type=MESH,
        )

    def sum_copy(way):
        source, target, mate = ((rsum, mate_rsum, col_mate), (csum, mate_csum, row_mate))[way]
        return pltpu.make_async_remote_copy(
            src_ref=source,
            dst_ref=target,
            send_sem=sum_send.at[way],
            recv_sem=sum_recv.at[way],
            device_id=mate,
            device_id_type=MESH,
        )

    for kind in range(4):
        @pl.when(links[kind][8])
        def _():
            links[kind][2][...] = jnp.zeros_like(links[kind][2])

    def head_send(kind, k):
        last, second = links[kind][9:]

        @pl.when(jnp.logical_not(both(last, second)))
        def _():
            swap(kind, k).start()

    def forward(kind, k):
        own, into, enter, leave, here, there = links[kind][:6]
        first, last, second = links[kind][8:]
        prior = jnp.logical_not(second)

        @pl.when(jnp.logical_not(both(last, prior)))
        def _():
            swap(kind, k).wait_recv()

        @pl.when(jnp.logical_not(first))
        def _():
            onward(kind, k).wait_recv()

        @pl.when(both(jnp.logical_not(last), second))
        def _():
            leave[k] = own[k] + here[k] * (into[k] + there[k] * enter[k])
            onward(kind, k).start()

        @pl.when(both(jnp.logical_not(last), prior))
        def _():
            leave[k] = into[k] + there[k] * (own[k] + here[k] * enter[k])
            onward(kind, k).start()

        @pl.when(second)
        def _():
            into[k] = into[k] + there[k] * enter[k]

        @pl.when(prior)
        def _():
            into[k] = enter[k]

    def lanes(k):
        return pl.ds(pl.multiple_of(k * LANES, LANES), LANES)

    def rates(cut):
        return jnp.exp(a_log_ref[:, cut]) * -math.log2(math.e)

    def flat(ref):
        return ref[...].reshape(cells, ref.shape[-1])

    def put(ref, cut, values):
        ref[:, :, cut] = values.reshape(tr, pad, values.shape[-1])

    def get(ref, cut):
        values = ref[:, :, cut]
        return values.reshape(cells, values.shape[-1])

    blocks = [slice(at, at + BLOCK) for at in range(0, width, BLOCK)]
    pad_ref[:, tc:, :] = jnp.zeros((tr, pad - tc, model), F32)
    pad_ref[:, :tc, :] = tokens_ref[...].astype(F32)
    tokens = flat(pad_ref).astype(BF16)
    for cut in blocks:
        x_pre = dot(tokens, w_in_ref[:, cut])
        put(x_pre_ref, cut, x_pre)
        put(x_ref, cut, (x_pre * sigmoid(x_pre)).astype(BF16).astype(F32))
    x_dbl = dot_transposed(flat(x_ref).astype(BF16), w_xproj_ref[...])
    xd_ref[:, : rank + 2 * states] = x_dbl
    dt_low = x_dbl[:, :rank].astype(BF16)
    for cut in blocks:
        dt_pre = dot(dt_low, w_dt_ref[:, cut]) + bias_ref[cut].reshape(1, BLOCK)
        step = jnp.maximum(dt_pre, 0.0) + jnp.log1p(jnp.exp(-jnp.abs(dt_pre)))
        put(dt_ref, cut, dt_pre)
        put(step_ref, cut, step)
        put(u_ref, cut, step * get(x_ref, cut))
    for cut in blocks:
        totals = jnp.zeros((pad, BLOCK), F32)
        for i in range(tr):
            steps = step_ref[i, :, cut]
            totals = totals + steps
            rsum[i : i + 1, cut] = jnp.sum(steps[:tc], axis=0, keepdims=True)
        csum[:, cut] = totals[:tc]
    peers = 2 + sum(jnp.where(edge, 0, 1) for edge, _ in edges)
    pl.semaphore_wait(barrier, peers)
    for way in range(2):
        sum_copy(way).start()
    pad_ref[:, :tc, :] = grad_ref[...].astype(F32)
    grads = flat(pad_ref).astype(BF16)
    for cut in blocks:
        z_pre = dot(tokens, w_in_ref[:, width + cut.start : width + cut.stop])
        gated = dot_transposed(grads, w_out_ref[cut, :])
        put(z_pre_ref, cut, z_pre)
        put(gated_ref, cut, gated)
        put(g_ref, cut, gated * (z_pre * sigmoid(z_pre)))
    for n in range(states):
        spot = pl.ds(n, cells, stride=states)
        for ref, first in ((b_ref, rank), (c_ref, rank + states)):
            column = xd_ref[:, first + n : first + n + 1]
            ref[spot, :] = jnp.broadcast_to(column, (cells, LANES))

    def tile_row(ref, i):
        size = pad * states
        return ref.at[pl.ds(pl.multiple_of(i * size, size), size)]

    def cell(j):
        return slice(j * states, (j + 1) * states)

    zero = jnp.zeros((states, LANES), F32)

    bacc_ref[...] = jnp.zeros_like(bacc_ref)
    cacc_ref[...] = jnp.zeros_like(cacc_ref)

    def local_ends(k):
        cut = lanes(k)
        rate = rates(cut)
        for i in range(tr):
            prow[k, i] = jnp.exp2(rate * rsum[i : i + 1, cut])
            mate_prow[k, i] = jnp.exp2(rate * mate_rsum[i : i + 1, cut])
        for j in range(tc):
            pcol[k, j] = jnp.exp2(rate * csum[j : j + 1, cut])
            mate_pcol[k, j] = jnp.exp2(rate * mate_csum[j : j + 1, cut])

        def line(count, terms):
            i = tr - 1 - count
            b_row, c_row = tile_row(b_ref, i), tile_row(c_ref, i)
            state = zero
            after = []
            for j in range(tc):
                d = jnp.exp2(rate * step_ref[i, j : j + 1, cut])
                decay[k, i, j] = d
                state = d * state + u_ref[i, j : j + 1, cut] * b_row[cell(j)]
                after.append(d * (terms[j] + g_ref[i, j : j + 1, cut] * c_row[cell(j)]))
            e1r[k, i] = state
            return tuple(after)

        terms = lax.fori_loop(0, tr, line, (zero,) * tc)
        for j in range(tc):
            e1c[k, j] = terms[j]
        head_send(0, k)
        head_send(1, k)

    def row_step(k):
        cut = lanes(k)
        forward(0, k)

        def down_line(i, states_in):
            b_row = tile_row(b_ref, i)
            state = in1r[k, i]
            after = []
            for j in range(tc):
                d = decay[k, i, j]
                state = d * state + u_ref[i, j : j + 1, cut] * b_row[cell(j)]
                rows[k, i, j] = state
                after.append(d * states_in[j] + state)
            return tuple(after)

        ends = lax.fori_loop(0, tr, down_line, (zero,) * tc)
        for j in range(tc):
            e2c[k, j] = ends[j]
        head_send(2, k)

    def col_step(k):
        cut = lanes(k)
        forward(1, k)

        def up_line(count, terms):
            i = tr - 1 - count
            c_row = tile_row(c_ref, i)
            term = zero
            after = [None] * tc
            for j in reversed(range(tc)):
                d = decay[k, i, j]
                adjoint = terms[j] + g_ref[i, j : j + 1, cut] * c_row[cell(j)]
                cols[k, i, j] = adjoint
                after[j] = d * adjoint
                term = d * (adjoint + term)
            e2r[k, i] = term
            return tuple(after)

        lax.fori_loop(0, tr, up_line, tuple(in1c[k, j] for j in range(tc)))
        head_send(3, k)

    def col_link(k):
        forward(2, k)

    def row_link(k):
        forward(3, k)

    def finish(k):
        cut = lanes(k)
        rate = rates(cut)
        for j in range(tc):
            fcar[j] = in2c[k, j]

        def last_line(i, carry):
            b_row, c_row = tile_row(b_ref, i), tile_row(c_ref, i)
            bacc_row, cacc_row = tile_row(bacc_ref, i), tile_row(cacc_ref, i)
            term = in2r[k, i]
            state = rows[k, i, tc - 1]
            for j in reversed(range(tc)):
                d = decay[k, i, j]
                adjoint = cols[k, i, j]
                before = in1r[k, i] if j == 0 else rows[k, i, j - 1]
                passed = d * fcar[j]
                full = passed + state
                fcar[j] = full
                total = adjoint + term
                term = d * total
                slope = adjoint * passed + term * before
                state = before
                sd_ref[i, j : j + 1, cut] = jnp.sum(slope * rate, axis=0, keepdims=True)
                rb_ref[i, j : j + 1, cut] = jnp.sum(total * b_row[cell(j)], axis=0, keepdims=True)
                out_ref[i, j : j + 1, cut] = jnp.sum(full * c_row[cell(j)], axis=0, keepdims=True)
                bacc_row[cell(j)] += total * u_ref[i, j : j + 1, cut]
                cacc_row[cell(j)] += full * g_ref[i, j : j + 1, cut]
            return carry

        lax.fori_loop(0, tr, last_line, 0)

    below, after = (n_row - 1 - r) // 2, (n_col - 1 - p) // 2

    def col_time(k):
        return START + LOCAL + COL_HOP * (p // 2) + ROW_HOP * (r // 2) + SPACE * k

    def row_time(k):
        return START + LOCAL + ROW_HOP * below + COL_HOP * after + SPACE * k

    table = (
        (local_ends, lambda k: START * k),
        (row_step, lambda k: START + 1 + COL_HOP * (p // 2) + START * k),
        (col_step, lambda k: START + 1 + ROW_HOP * below + SPACE * k),
        (col_link, col_time),
        (row_link, row_time),
        (finish, lambda k: jnp.maximum(col_time(k), row_time(k)) + 1),
    )

    def slot(_, counts):
        times = [
            jnp.where(k < chunks, time(k), NEVER) for k, (_, time) in zip(counts, table)
        ]
        best = functools.reduce(jnp.minimum, times)
        free, after_counts = jnp.int32(1), []
        for k, due, (step, _) in zip(counts, times, table):
            hit = jnp.where(due == best, free, 0)
            free = free - hit
            pl.when(hit == 1)(functools.partial(step, k))
            after_counts.append(k + hit)
        return tuple(after_counts)

    for way in range(2):
        sum_copy(way).wait_recv()
    lax.fori_loop(0, len(table) * chunks, slot, (jnp.int32(0),) * len(table))

    narrow = jnp.zeros((cells, 2 * states), F32)
    lane = lax.broadcasted_iota(jnp.int32, (LANES, 2 * states), 1)
    for n in range(states):
        spot = pl.ds(n, cells, stride=states)
        for ref, at in ((bacc_ref, n), (cacc_ref, states + n)):
            pick = jnp.where(lane == at, 1.0, 0.0).astype(BF16)
            narrow = narrow + dot(ref[spot, :].astype(BF16), pick)
    low_grad = jnp.zeros((cells, rank), F32)
    layer = jnp.zeros((cells, model), F32)
    for cut in blocks:
        x, z_pre, dt_pre = get(x_ref, cut), get(z_pre_ref, cut), get(dt_ref, cut)
        scan_out = get(out_ref, cut) + skip_ref[cut].reshape(1, BLOCK) * x
        layer = layer + dot((scan_out * (z_pre * sigmoid(z_pre))).astype(BF16), w_out_ref[cut, :])
        put(proj_ref, slice(width + cut.start, width + cut.stop),
            get(gated_ref, cut) * scan_out * silu_grad(z_pre))
        step_grad = get(sd_ref, cut) * math.log(2.0) + get(rb_ref, cut) * x
        low_grad = low_grad + dot_transposed(
            (step_grad / (1.0 + jnp.exp(-dt_pre))).astype(BF16), w_dt_ref[:, cut]
        )
    layer_ref[...] = layer.reshape(tr, pad, model)[:, :tc, :].astype(BF16)
    xd_ref[:, :rank] = low_grad
    xd_ref[:, rank : rank + 2 * states] = narrow
    dbl_grad = xd_ref[:, : rank + 2 * states].astype(BF16)
    for cut in blocks:
        x_grad = (
            get(rb_ref, cut) * get(step_ref, cut) + get(g_ref, cut) * skip_ref[cut].reshape(1, BLOCK)
            + dot(dbl_grad, w_xproj_ref[:, cut])
        )
        put(proj_ref, cut, x_grad * silu_grad(get(x_pre_ref, cut)))
    proj = flat(proj_ref).astype(BF16)
    for at in range(0, model, BLOCK):
        token_grad = dot_transposed(proj, w_in_ref[at : at + BLOCK, :])
        token_grad_ref[:, :, at : at + BLOCK] = (
            token_grad.reshape(tr, pad, BLOCK)[:, :tc, :].astype(BF16)
        )

    for way in range(2):
        sum_copy(way).wait_send()
    for kind in range(4):
        last, second = links[kind][9:]

        @pl.when(jnp.logical_not(last))
        def _():
            @pl.loop(0, chunks)
            def _(k):
                onward(kind, k).wait_send()

        @pl.when(jnp.logical_not(both(last, second)))
        def _():
            @pl.loop(0, chunks)
            def _(k):
                swap(kind, k).wait_send()


def body(mesh_shape, tokens, w_in, w_xproj, w_dt, dt_bias, a_log, d_skip, w_out, out_grad):
    tr, tc, model = tokens.shape
    rank, width = w_dt.shape
    states = a_log.shape[0]
    chunks = width // LANES
    pad = -(-tc // 16) * 16
    sizes = (mesh_shape["row"], mesh_shape["col"], tr, tc, chunks, states, rank)
    grid_buf = pltpu.VMEM((chunks, tr, tc, states, LANES), F32)
    row_buf = pltpu.VMEM((chunks, tr, states, LANES), F32)
    col_buf = pltpu.VMEM((chunks, tc, states, LANES), F32)
    wide = pltpu.VMEM((tr, pad, width), F32)
    acc = pltpu.VMEM((tr * pad * states, LANES), F32)
    out = jax.ShapeDtypeStruct((tr, tc, model), BF16)
    return pl.pallas_call(
        functools.partial(layer_kernel, sizes),
        out_shape=(out, out),
        in_specs=[pl.BlockSpec(memory_space=pltpu.VMEM)] * 9,
        out_specs=(pl.BlockSpec(memory_space=pltpu.VMEM),) * 2,
        scratch_shapes=[
            pltpu.VMEM((tr, pad, model), F32)] + [wide] * 11 + [
            pltpu.VMEM((tr, pad, 2 * width), F32), pltpu.VMEM((tr * pad, LANES), F32),
            acc, acc, acc, acc,
            grid_buf, grid_buf, grid_buf, row_buf, col_buf, row_buf, col_buf,
        ] + [row_buf, col_buf, row_buf, col_buf] * 4 + [
            pltpu.VMEM((tc, states, LANES), F32),
            pltpu.VMEM((tr, width), F32), pltpu.VMEM((tc, width), F32),
            pltpu.VMEM((tr, width), F32), pltpu.VMEM((tc, width), F32),
        ] + [pltpu.SemaphoreType.DMA((4, chunks))] * 4 + [pltpu.SemaphoreType.DMA((2,))] * 2 + [
        ],
        compiler_params=pltpu.CompilerParams(
            collective_id=0, has_side_effects=True, vmem_limit_bytes=60 * 1024 * 1024
        ),
    )(
        tokens, w_in, w_xproj.T, w_dt, dt_bias, a_log, d_skip, w_out, out_grad,
    )


def solution(mesh):
    return jax.shard_map(
        functools.partial(body, dict(mesh.shape)),
        mesh=mesh,
        in_specs=(P("row", "col", None), P(), P(), P(), P(), P(), P(), P(), P("row", "col", None)),
        out_specs=(P("row", "col", None), P("row", "col", None)),
        check_vma=False,
    )
```
